128 devices in a mesh: rep: 16 (over x, y), shard: 8 (over z, core).
Axes of the slice: x: 4, y: 4, z: 4, core: 2. Of those that a mesh axis runs over, the one named last changes fastest.
Arguments:
- tokens: bfloat16 [16384, 1024], P(('rep', 'shard')), may hold values from -24 to 24
- cotangent: bfloat16 [16384, 1024], P(('rep', 'shard')), may hold values from -6 to 6
- lengths: int32 [16, 3], P('rep'), may hold values from 1 to 898, 1024 in all within a row
- qkv_proj: float32 [1024, 2048], P(('rep', 'shard')), may hold values from -0.1875 to 0.1875
- out_proj: float32 [1024, 1024], P(('rep', 'shard')), may hold values from -3 to 3
- gate_proj: float32 [1024, 9216], P(('rep', 'shard')), may hold values from -0.1875 to 0.1875
- down_proj: float32 [4608, 1024], P(('rep', 'shard')), may hold values from -0.09375 to 0.09375
- norm_gains: float32 [2176], P(('rep', 'shard')), may hold values from 0.5 to 1.5
- qkv_first: float32 [1024, 2048], P(('rep', 'shard')), may hold values from -40 to 40
- out_first: float32 [1024, 1024], P(('rep', 'shard')), may hold values from -6 to 6
- gate_first: float32 [1024, 9216], P(('rep', 'shard')), may hold values from -24 to 24
- down_first: float32 [4608, 1024], P(('rep', 'shard')), may hold values from -48 to 48
- gain_first: float32 [2176], P(('rep', 'shard')), may hold values from -64 to 64
- qkv_second: float32 [1024, 2048], P(('rep', 'shard')), may hold values from 212.992 to 868.352
- out_second: float32 [1024, 1024], P(('rep', 'shard')), may hold values from 4.16 to 16.8
- gate_second: float32 [1024, 9216], P(('rep', 'shard')), may hold values from 62.2592 to 245.76
- down_second: float32 [4608, 1024], P(('rep', 'shard')), may hold values from 311.296 to 1245.184
- gain_second: float32 [2176], P(('rep', 'shard')), may hold values from 425.984 to 1638.4
Outputs:
- block_output: float32 [16384, 1024], P(('rep', 'shard'))
- input_grad: float32 [16384, 1024], P(('rep', 'shard'))
- qkv_next: float32 [1024, 2048], P(('rep', 'shard'))
- qkv_mean: float32 [1024, 2048], P(('rep', 'shard'))
- qkv_square: float32 [1024, 2048], P(('rep', 'shard'))
- out_next: float32 [1024, 1024], P(('rep', 'shard'))
- out_mean: float32 [1024, 1024], P(('rep', 'shard'))
- out_square: float32 [1024, 1024], P(('rep', 'shard'))
- gate_next: float32 [1024, 9216], P(('rep', 'shard'))
- gate_mean: float32 [1024, 9216], P(('rep', 'shard'))
- gate_square: float32 [1024, 9216], P(('rep', 'shard'))
- down_next: float32 [4608, 1024], P(('rep', 'shard'))
- down_mean: float32 [4608, 1024], P(('rep', 'shard'))
- down_square: float32 [4608, 1024], P(('rep', 'shard'))
- gain_next: float32 [2176], P(('rep', 'shard'))
- gain_mean: float32 [2176], P(('rep', 'shard'))
- gain_square: float32 [2176], P(('rep', 'shard'))
The draws below stay inside these ranges and needn't reach their ends.
Inputs may be any that keep to these rules, and one draw needn't show every extreme that they name: Each row holds the 3 lengths of the documents packed in order into one sequence; they sum to 1024, and one of them is exactly 898.
All inputs are finite; a program needn't handle non-finite values.
Results may differ from the reference program's by a relative error of at most 0.02.
Values may be sent and summed in bfloat16 or wider, within the bound.
No kernel may reach another device: no remote copies, remote signals or barrier semaphores. Data moves between devices by JAX's collectives and lax.ppermute only.
A program may use at most 192 MiB of HBM per device.

```python
import math
import jax
import jax.numpy as jnp
import numpy as np
from jax import lax

D = 1024
FF = 4608
HQ = 16
KEY_VALUE_HEADS = 8
HEAD_SIZE = 64
PACKED_TOKENS = 1024
NDOC = 3
STEP = 10
QUERY_FEATURES = 1024
KEY_FEATURES = 512
QUERY_PER_KEY = 2
GAINS = 2176
TOKENS = 16384
WO_FAN = 4
LONGEST = 898
N_REP = 16


def raised(array, rng, source, target, shards_of, factor):
    owner, partner = [(jnp.arange(array.shape[position]) // (array.shape[position] // shards_of)).reshape([-1 if axis == position else 1 for axis in range(array.ndim)]) for position in (source, target)]
    chosen = jax.random.permutation(rng, shards_of)[partner]
    strong = (owner == chosen) | (owner == (partner + shards_of // 2) % shards_of)
    return jnp.where(strong, factor * array, array)


def level_of(key, shape, pieces, least, high):
    def one(position, blocks):
        draws = jax.random.uniform(jax.random.fold_in(jax.random.fold_in(key, 6), position), (blocks,), jnp.float32, least / len(pieces), high / len(pieces))
        return jnp.repeat(jnp.exp(draws), shape[position] // blocks).reshape((-1,) + (1,) * (len(shape) - position - 1))

    loudness = one(*pieces[0])
    for cut in pieces[1:]:
        loudness = loudness * one(*cut)
    return loudness


def split_up(number_of, total, limit, slope):
    loads = [(1 << 20) // math.isqrt(standing ** slope) + 1 for standing in range(2, number_of + 1)]
    spare, counts = total - limit - (number_of - 1), [1] * (number_of - 1)
    while spare > 0:
        candidates = [i for i in range(number_of - 1) if counts[i] < limit]
        mass, left = sum([loads[i] for i in candidates]), spare
        for i in candidates:
            addition = min(limit - counts[i], max(1, left * loads[i] // mass), spare)
            counts[i] = counts[i] + addition
            spare = spare - addition
    return np.array([limit] + counts)


def uneven(own_key, amount, total, bound, skew):
    if amount == 2:
        one = jax.random.randint(own_key, (), max(1, total - bound), min(bound, total - 1) + 1)
        return jnp.stack([one, total - one])
    sizes = jnp.asarray(split_up(amount, total, bound, skew), jnp.int32)
    couples = (amount - 1) // 2
    giver, sink = sizes[1:1 + 2 * couples:2], sizes[2:2 + 2 * couples:2]
    slack = jnp.minimum(giver - 1, bound - sink)
    shifted = jax.random.randint(jax.random.fold_in(own_key, 1), (couples,), 0, 1 << 20) % (slack + 1)
    sizes = sizes.at[1:1 + 2 * couples:2].set(giver - shifted).at[2:2 + 2 * couples:2].set(sink + shifted)
    return sizes[jax.random.permutation(jax.random.fold_in(own_key, 2), amount)]


def normal_values(stream_key, extent, spread, reach, cuts=(), kind=jnp.bfloat16):
    entries = jax.random.normal(stream_key, extent, jnp.float32) * spread
    if len(cuts) > 0:
        entries = level_of(stream_key, extent, cuts, -0.22, 0.18) * entries
    return jnp.clip(entries, min=-reach, max=reach).astype(kind)


def gaussian_with(stream_key, extent, spread, bound, cuts, heavy, kind=jnp.bfloat16):
    values = spread * jax.random.normal(stream_key, extent, jnp.float32)
    if cuts:
        values = values * level_of(stream_key, extent, cuts, -0.22, 0.18)
    return jnp.clip(raised(values, jax.random.fold_in(stream_key, 3), *heavy), -bound, bound).astype(kind)


def setup_inputs(seed: int = 0) -> dict:
    key_of = jax.random.split(jax.random.key(seed), 19)
    tokens = gaussian_with(key_of[0], (TOKENS, D), 1.0, 24.0, ((0, 128),), (0, 1, 128, 5.5))
    cotangent = normal_values(key_of[1], (TOKENS, D), 1.0, 6.0, ((0, 128),))
    lengths = jax.vmap(lambda own: uneven(own, NDOC, PACKED_TOKENS, LONGEST, 2))(jax.random.split(key_of[2], N_REP)).reshape((N_REP, NDOC)).astype(jnp.int32)
    qkv_proj = normal_values(key_of[3], (D, QUERY_FEATURES + 2 * KEY_FEATURES), D ** -0.5, 0.1875, ((0, 128),), jnp.float32)
    out_proj = normal_values(key_of[4], (QUERY_FEATURES, D), WO_FAN ** -0.5, 3.0, ((0, 128),), jnp.float32)
    gate_proj = normal_values(key_of[5], (D, 2 * FF), D ** -0.5, 0.1875, ((0, 128),), jnp.float32)
    down_proj = normal_values(key_of[6], (FF, D), FF ** -0.5, 0.09375, ((0, 128),), jnp.float32)
    norm_gains = jnp.clip(1.0 + 0.1 * jax.random.normal(key_of[7], (GAINS,), jnp.float32), 0.5, 1.5)
    qkv_first = normal_values(key_of[8], (D, QUERY_FEATURES + 2 * KEY_FEATURES), (0.055 * TOKENS ** 0.5), 40.0, ((0, 128),), jnp.float32)
    out_first = normal_values(key_of[9], (QUERY_FEATURES, D), (0.25 * N_REP ** 0.5), 6.0, ((0, 128),), jnp.float32)
    gate_first = normal_values(key_of[10], (D, 2 * FF), (0.03 * TOKENS ** 0.5), 24.0, ((0, 128),), jnp.float32)
    down_first = normal_values(key_of[11], (FF, D), (0.067 * TOKENS ** 0.5), 48.0, ((0, 128),), jnp.float32)
    gain_first = normal_values(key_of[12], (GAINS,), (0.078 * TOKENS ** 0.5), 64.0, ((0, 128),), jnp.float32)
    qkv_second = jnp.clip(jnp.exp(math.log(868.352) - 1.40534252 * jax.random.uniform(key_of[13], (D, QUERY_FEATURES + 2 * KEY_FEATURES), jnp.float32) ** level_of(key_of[13], (D, QUERY_FEATURES + 2 * KEY_FEATURES), ((0, 128),), -0.2, 0.2)), 212.992, 868.352)
    out_second = jnp.clip(jnp.exp(math.log(16.8) - 1.3958638 * jax.random.uniform(key_of[14], (QUERY_FEATURES, D), jnp.float32) ** level_of(key_of[14], (QUERY_FEATURES, D), ((0, 128),), -0.2, 0.2)), 4.16, 16.8)
    gate_second = jnp.clip(jnp.exp(math.log(245.76) - 1.3730491 * jax.random.uniform(key_of[15], (D, 2 * FF), jnp.float32) ** level_of(key_of[15], (D, 2 * FF), ((0, 128),), -0.2, 0.2)), 62.2592, 245.76)
    down_second = jnp.clip(jnp.exp(math.log(1245.184) - 1.3862944 * jax.random.uniform(key_of[16], (FF, D), jnp.float32) ** level_of(key_of[16], (FF, D), ((0, 128),), -0.2, 0.2)), 311.296, 1245.184)
    gain_second = jnp.clip(jnp.exp(math.log(1638.4) - 1.34707364 * jax.random.uniform(key_of[17], (GAINS,), jnp.float32) ** level_of(key_of[17], (GAINS,), ((0, 128),), -0.2, 0.2)), 425.984, 1638.4)
    return {"tokens": tokens, "cotangent": cotangent, "lengths": lengths, "qkv_proj": qkv_proj, "out_proj": out_proj, "gate_proj": gate_proj, "down_proj": down_proj, "norm_gains": norm_gains, "qkv_first": qkv_first, "out_first": out_first, "gate_first": gate_first, "down_first": down_first, "gain_first": gain_first, "qkv_second": qkv_second, "out_second": out_second, "gate_second": gate_second, "down_second": down_second, "gain_second": gain_second}


norm_eps = 1e-05
theta = 1000000.0
beta_one = 0.9
beta_two = 0.95
adam_eps = 1e-08
decay = 0.1
rate_scale = 2.0
gain_rate = 1.0
masked_score = -1e+30
highest = lax.Precision.HIGHEST

@jax.custom_vjp
def reduced_precision(v):
    return lax.optimization_barrier(v.astype(jnp.bfloat16)).astype(jnp.float32)

@jax.custom_vjp
def reduced_precision_grad(v):
    return v

def low_keep(v):
    return (reduced_precision(v), None)

def low_pass(kept, grad):
    return (grad,)

def back_keep(v):
    return (v, None)

def back_low(kept, grad):
    return (reduced_precision(grad),)
reduced_precision.defvjp(low_keep, low_pass)
reduced_precision_grad.defvjp(back_keep, back_low)

def row_rms_norm(field, gain):
    scale = lax.rsqrt(lax.optimization_barrier(jnp.mean(field * field, axis=-1, keepdims=True)) + norm_eps)
    return field * scale * gain

def document_info(lengths_row, index):
    ends = jnp.cumsum(lengths_row)
    passed = ends[None, :] <= index[:, None]
    docs = lax.optimization_barrier(jnp.sum(passed.astype(jnp.int32), axis=1))
    starts = lax.optimization_barrier(jnp.sum(jnp.where(passed, lengths_row[None, :], 0), axis=1))
    return (docs, (index - starts).astype(jnp.int32))

def rotation_tables(places):
    half = HEAD_SIZE // 2
    freqs = theta ** (-(jnp.arange(half, dtype=jnp.float32) * 2.0) / HEAD_SIZE)
    angles = places.astype(jnp.float32)[:, None] * freqs[None, :]
    return (jnp.cos(angles), jnp.sin(angles))

def apply_rotary(field, cosine_table, sine_table):
    half = field.shape[-1] // 2
    first = field[..., :half]
    second = field[..., half:]
    cos_rows = cosine_table[:, None, :]
    sin_rows = sine_table[:, None, :]
    return jnp.concatenate([first * cos_rows - second * sin_rows, second * cos_rows + first * sin_rows], axis=-1)

def sequence_forward(lowered, inputs, lengths_row):
    qkv_w, out_w, gate_w, down_w, gain_all = lowered
    index = jnp.arange(PACKED_TOKENS, dtype=jnp.int32)
    docs, places = document_info(lengths_row, index)
    cosine_table, sine_table = rotation_tables(places)
    gain_attn = gain_all[:D]
    query_norm_gain = gain_all[D:D + HEAD_SIZE]
    gain_key = gain_all[D + HEAD_SIZE:D + 2 * HEAD_SIZE]
    gain_ffn = gain_all[D + 2 * HEAD_SIZE:]
    normed = reduced_precision(row_rms_norm(inputs, gain_attn))
    projected_rows = jnp.dot(normed, qkv_w, precision=highest)
    query_unnormed = reduced_precision_grad(projected_rows[:, :QUERY_FEATURES]).reshape(PACKED_TOKENS, HQ, HEAD_SIZE)
    key_unnormed = reduced_precision_grad(projected_rows[:, QUERY_FEATURES:QUERY_FEATURES + KEY_FEATURES]).reshape(PACKED_TOKENS, KEY_VALUE_HEADS, HEAD_SIZE)
    value_rows = reduced_precision(reduced_precision_grad(projected_rows[:, QUERY_FEATURES + KEY_FEATURES:])).reshape(PACKED_TOKENS, KEY_VALUE_HEADS, HEAD_SIZE)
    query_rows = reduced_precision(apply_rotary(row_rms_norm(query_unnormed, query_norm_gain), cosine_table, sine_table)).reshape(PACKED_TOKENS, KEY_VALUE_HEADS, QUERY_PER_KEY, HEAD_SIZE)
    key_rows = reduced_precision(apply_rotary(row_rms_norm(key_unnormed, gain_key), cosine_table, sine_table))
    scores = reduced_precision_grad(jnp.einsum('tgjd,sgd->gjts', query_rows, key_rows, precision=highest) * HEAD_SIZE ** (-0.5))
    allowed = (index[None, :] <= index[:, None]) & (docs[None, :] == docs[:, None])
    probs = jax.nn.softmax(jnp.where(allowed, scores, masked_score), axis=-1)
    mixed = jnp.einsum('gjts,sgd->tgjd', reduced_precision(probs), value_rows, precision=highest).reshape(PACKED_TOKENS, QUERY_FEATURES)
    mixed = reduced_precision_grad(reduced_precision(mixed))
    residual = inputs + reduced_precision_grad(jnp.dot(mixed, out_w, precision=highest))
    normed_two = reduced_precision(row_rms_norm(residual, gain_ffn))
    both = jnp.dot(normed_two, gate_w, precision=highest)
    gate = reduced_precision_grad(both[:, :FF])
    upper = reduced_precision_grad(both[:, FF:])
    hidden = reduced_precision(jax.nn.silu(gate) * upper)
    return residual + reduced_precision_grad(jnp.dot(hidden, down_w, precision=highest))

def adamw(weight, grad, first, second, rate, weight_decay):
    new_first = beta_one * first + (1.0 - beta_one) * grad
    new_second = beta_two * second + (1.0 - beta_two) * grad * grad
    step_size = new_first / (1.0 - beta_one ** STEP) / (jnp.sqrt(new_second / (1.0 - beta_two ** STEP)) + adam_eps)
    return (weight - rate * (step_size + weight_decay * weight), new_first, new_second)

def reference(tokens, cotangent, lengths, qkv_proj, out_proj, gate_proj, down_proj, norm_gains, qkv_first, out_first, gate_first, down_first, gain_first, qkv_second, out_second, gate_second, down_second, gain_second):
    params = (qkv_proj.astype(jnp.float32), out_proj.astype(jnp.float32), gate_proj.astype(jnp.float32), down_proj.astype(jnp.float32), norm_gains.astype(jnp.float32))
    inputs = tokens.astype(jnp.float32).reshape(N_REP, PACKED_TOKENS, D)

    def forward(weights, stream):
        lowered = tuple((reduced_precision(w) for w in weights))
        checked = jax.checkpoint(sequence_forward)

        def scan_body(carry, item):
            return (carry, checked(lowered, item[0], item[1]))
        unused, outputs = lax.scan(scan_body, jnp.zeros((), jnp.float32), (stream, lengths))
        return outputs
    outputs, pull = jax.vjp(forward, params, inputs)
    grads, input_grads = pull(cotangent.astype(jnp.float32).reshape(N_REP, PACKED_TOKENS, D))
    rates = (rate_scale * D ** (-0.5), rate_scale * WO_FAN ** (-0.5), rate_scale * D ** (-0.5), rate_scale * FF ** (-0.5), gain_rate)
    decays = (decay, decay, decay, decay, 0.0)
    firsts = (qkv_first, out_first, gate_first, down_first, gain_first)
    seconds = (qkv_second, out_second, gate_second, down_second, gain_second)
    results = []
    for number in range(5):
        results.extend(adamw(params[number], grads[number], firsts[number], seconds[number], rates[number], decays[number]))
    return (outputs.reshape(TOKENS, D), input_grads.reshape(TOKENS, D), results[0], results[1], results[2], results[3], results[4], results[5], results[6], results[7], results[8], results[9], results[10], results[11], results[12], results[13], results[14])
```

```python
import jax
import jax.numpy as jnp
from jax import lax
from jax.experimental import pallas as pl
from jax.experimental.pallas import tpu as pltpu
from jax.sharding import PartitionSpec as P

D = 1024
FF = 4608
HEAD_SIZE = 64
STEP = 10
QUERY_FEATURES = 1024
KEY_FEATURES = 512
WO_FAN = 4

norm_eps = 1e-05
theta = 1000000.0
beta_one = 0.9
beta_two = 0.95
adam_eps = 1e-08
decay = 0.1
rate_scale = 2.0
gain_rate = 1.0
masked_score = -1e30

SHARDS = 8
CHIPS = 4
FF_OWN = FF // SHARDS
FF_PAD = 640
ROWS_FF_PAD = 40
QUERY_BLOCK = 256
score_scale = HEAD_SIZE ** (-0.5)
low = jnp.bfloat16
wide = jnp.float32
sibling = [(i, i ^ 1) for i in range(SHARDS)]


def from_chip(k):
    return [(i, ((i // 2 - k) % CHIPS) * 2 + i % 2) for i in range(SHARDS)]


def gather_rows(rows):
    parts = [rows] + [lax.ppermute(rows, "shard", from_chip(k)) for k in range(1, CHIPS)]
    mine = jnp.concatenate(parts, axis=0)
    other = lax.ppermute(mine, "shard", sibling)
    return jnp.concatenate([mine, other], axis=0)


def scatter_rows(mine, other):
    count = mine.shape[0] // CHIPS
    got = lax.ppermute(other.astype(low), "shard", sibling)
    both = mine + got.astype(wide)
    sent = both.astype(low)
    total = both[:count]
    for k in (2, 1, 3):
        total = total + lax.ppermute(
            sent[k * count : (k + 1) * count], "shard", from_chip(-k)
        ).astype(wide)
    return total


def norm_pieces(field):
    scale = lax.rsqrt(jnp.mean(field * field, axis=-1, keepdims=True) + norm_eps)
    return field * scale, scale


def norm_back(incoming_grad, normed, scale, gain):
    gain_grad = jnp.sum(incoming_grad * normed, axis=0)
    scaled = incoming_grad * gain
    inner = jnp.mean(scaled * normed, axis=-1, keepdims=True)
    return gain_grad, scale * (scaled - normed * inner)


def sequence_info(lengths_row, index):
    ends = jnp.cumsum(lengths_row)
    passed = ends[None, :] <= index[:, None]
    return jnp.sum(jnp.where(passed, lengths_row[None, :], 0), axis=1)


def rotation_tables(places):
    half = HEAD_SIZE // 2
    freqs = theta ** (-(jnp.arange(half, dtype=wide) * 2.0) / HEAD_SIZE)
    angles = places.astype(wide)[:, None] * freqs[None, :]
    cos, sin = jnp.cos(angles), jnp.sin(angles)
    return jnp.concatenate([cos] * 4, axis=1), jnp.concatenate([-sin, sin, -sin, sin], axis=1)


def lanes(rows):
    return lax.broadcasted_iota(jnp.int32, (rows, 2 * HEAD_SIZE), 1)


def partner(field):
    first = lanes(field.shape[0]) % HEAD_SIZE < HEAD_SIZE // 2
    return jnp.where(first, pltpu.roll(field, 96, 1), pltpu.roll(field, 32, 1))


def left_mean(field):
    left = lanes(field.shape[0]) < HEAD_SIZE
    return jnp.sum(jnp.where(left, field, 0.0), axis=1, keepdims=True) / HEAD_SIZE


def head_means(field):
    left = lanes(field.shape[0]) < HEAD_SIZE
    one = jnp.sum(jnp.where(left, field, 0.0), axis=1, keepdims=True) / HEAD_SIZE
    two = jnp.sum(jnp.where(left, 0.0, field), axis=1, keepdims=True) / HEAD_SIZE
    return jnp.where(left, one, two)


def swap_heads(field):
    return pltpu.roll(field, HEAD_SIZE, 1)


def stack_heads(block):
    left = (lax.broadcasted_iota(jnp.int32, (1, 2 * HEAD_SIZE), 1) < HEAD_SIZE).astype(wide)
    return jnp.concatenate([block * left.astype(low), block * (1.0 - left).astype(low)], axis=0)


def allowed_keys(start_ref, block, keys):
    begin = start_ref[block * QUERY_BLOCK : (block + 1) * QUERY_BLOCK, :]
    begin = jnp.concatenate([begin, begin], axis=0)
    row = lax.broadcasted_iota(jnp.int32, (2 * QUERY_BLOCK, keys), 0)
    row = block * QUERY_BLOCK + jnp.where(row >= QUERY_BLOCK, row - QUERY_BLOCK, row)
    col = lax.broadcasted_iota(jnp.int32, (2 * QUERY_BLOCK, keys), 1)
    return (col >= begin) & (col <= row)


def dot_last(one, two):
    return lax.dot_general(one, two, (((1,), (1,)), ((), ())), preferred_element_type=wide)


def dot_first(one, two):
    return lax.dot_general(one, two, (((0,), (0,)), ((), ())), preferred_element_type=wide)


def forward_kernel(
    place_ref, proj_ref, cos_ref, sin_ref, start_ref, gain_ref,
    out_ref, query_ref, key_ref, value_ref, shift_ref, mixed_ref,
):
    count = proj_ref.shape[0] // SHARDS
    left = lanes(count) < HEAD_SIZE
    gain_query = gain_ref[:, :128]
    gain_key = gain_ref[:, 128:]
    for chunk in range(SHARDS):
        place = pl.multiple_of(place_ref[chunk], 128)
        rows = slice(chunk * count, (chunk + 1) * count)
        there = pl.ds(place, count)
        cos, sin = cos_ref[there, :], sin_ref[there, :]
        query = proj_ref[rows, :128]
        query = query * lax.rsqrt(head_means(query * query) + norm_eps) * gain_query
        query = (query * cos + partner(query) * sin).astype(low)
        query_ref[there, :] = query * jnp.asarray(score_scale, low)
        both = proj_ref[rows, 128:]
        key = both * lax.rsqrt(left_mean(both * both) + norm_eps) * gain_key
        key = key * cos + partner(key) * sin
        both = jnp.where(left, key, both)
        turned = swap_heads(both)
        key_ref[there, :] = jnp.where(left, both, turned).astype(low)
        value_ref[there, :] = jnp.where(left, turned, both).astype(low)
    half = lanes(QUERY_BLOCK) < HEAD_SIZE
    for block in range(proj_ref.shape[0] // QUERY_BLOCK):
        keys = (block + 1) * QUERY_BLOCK
        span = slice(block * QUERY_BLOCK, keys)
        query = stack_heads(query_ref[span, :])
        raw = dot_last(query, key_ref[:keys, :])
        raw = jnp.where(allowed_keys(start_ref, block, keys), raw, masked_score)
        top = jnp.max(raw, axis=1, keepdims=True)
        weight = jnp.exp(raw - top)
        total = jnp.sum(weight, axis=1, keepdims=True)
        probs = (weight * (1.0 / total)).astype(low)
        mixed = jnp.dot(probs, value_ref[:keys, :], preferred_element_type=wide)
        mixed_ref[span, :] = jnp.where(half, mixed[:QUERY_BLOCK], mixed[QUERY_BLOCK:])
        shift_ref[2 * block * QUERY_BLOCK : 2 * keys, :] = top + jnp.log(total)
    for chunk in range(SHARDS):
        place = pl.multiple_of(place_ref[chunk], 128)
        out_ref[chunk * count : (chunk + 1) * count, :] = mixed_ref[pl.ds(place, count), :].astype(low)


def backward_kernel(
    place_ref, proj_ref, cos_ref, sin_ref, start_ref, gain_ref, query_ref, key_ref, value_ref,
    shift_ref, incoming_ref, out_ref, gain_grad_ref, back_ref, query_grad_ref, key_grad_ref,
    value_grad_ref,
):
    count = proj_ref.shape[0] // SHARDS
    left = lanes(count) < HEAD_SIZE
    gain_query = gain_ref[:, :128]
    gain_key = gain_ref[:, 128:]
    for chunk in range(SHARDS):
        place = pl.multiple_of(place_ref[chunk], 128)
        back_ref[pl.ds(place, count), :] = incoming_ref[chunk * count : (chunk + 1) * count, :]
    key_grad_ref[...] = jnp.zeros_like(key_grad_ref)
    value_grad_ref[...] = jnp.zeros_like(value_grad_ref)
    half = lanes(QUERY_BLOCK) < HEAD_SIZE
    for block in range(proj_ref.shape[0] // QUERY_BLOCK):
        keys = (block + 1) * QUERY_BLOCK
        span = slice(block * QUERY_BLOCK, keys)
        query = stack_heads(query_ref[span, :])
        back = stack_heads(back_ref[span, :])
        raw = dot_last(query, key_ref[:keys, :])
        shift = shift_ref[2 * block * QUERY_BLOCK : 2 * keys, :]
        probs = jnp.where(allowed_keys(start_ref, block, keys), jnp.exp(raw - shift), 0.0)
        prob_grad = dot_last(back, value_ref[:keys, :])
        spread = jnp.sum(probs * prob_grad, axis=1, keepdims=True)
        score_grad = (probs * (prob_grad - spread)).astype(low)
        query_grad = jnp.dot(score_grad, key_ref[:keys, :], preferred_element_type=wide)
        query_grad_ref[span, :] = score_scale * jnp.where(
            half, query_grad[:QUERY_BLOCK], query_grad[QUERY_BLOCK:]
        )
        key_grad_ref[:keys, :] += dot_first(score_grad, query)
        value_grad_ref[:keys, :] += dot_first(probs.astype(low), back)
    gain_query_grad = jnp.zeros((1, 128), wide)
    gain_key_grad = jnp.zeros((1, 128), wide)
    for chunk in range(SHARDS):
        place = pl.multiple_of(place_ref[chunk], 128)
        rows = slice(chunk * count, (chunk + 1) * count)
        there = pl.ds(place, count)
        cos, sin = cos_ref[there, :], sin_ref[there, :]
        query = proj_ref[rows, :128]
        scale = lax.rsqrt(head_means(query * query) + norm_eps)
        query = query * scale
        grad = query_grad_ref[there, :]
        grad = grad * cos - partner(grad) * sin
        gain_query_grad += jnp.sum(grad * query, axis=0, keepdims=True)
        grad = grad * gain_query
        out_ref[rows, :128] = (scale * (grad - query * head_means(grad * query))).astype(low)
        key = proj_ref[rows, 128:]
        scale = lax.rsqrt(left_mean(key * key) + norm_eps)
        key = key * scale
        grad = key_grad_ref[there, :]
        grad = grad + swap_heads(grad)
        grad = grad * cos - partner(grad) * sin
        gain_key_grad += jnp.sum(grad * key, axis=0, keepdims=True)
        grad = grad * gain_key
        grad = scale * (grad - key * left_mean(grad * key))
        value_grad = value_grad_ref[there, :]
        value_grad = value_grad + swap_heads(value_grad)
        out_ref[rows, 128:] = jnp.where(left, grad, value_grad).astype(low)
    gain_grad_ref[:, :128] = gain_query_grad
    gain_grad_ref[:, 128:] = gain_key_grad


def in_vmem(count):
    return [pl.BlockSpec(memory_space=pltpu.VMEM)] * count


def attention_forward(place, projected, cos, sin, start, gain):
    rows = projected.shape[0]
    return pl.pallas_call(
        forward_kernel,
        out_shape=[jax.ShapeDtypeStruct((rows, 128), low)] * 4
        + [jax.ShapeDtypeStruct((2 * rows, 1), wide)],
        in_specs=[pl.BlockSpec(memory_space=pltpu.SMEM)] + in_vmem(5),
        out_specs=in_vmem(5),
        scratch_shapes=[pltpu.VMEM((rows, 128), wide)],
        compiler_params=pltpu.CompilerParams(vmem_limit_bytes=40 * 2**20),
        cost_estimate=pl.CostEstimate(
            flops=10**9, bytes_accessed=5 * 2**20, transcendentals=2 * 10**6
        ),
        name="attention_forward",
    )(place, projected, cos, sin, start, gain)


def attention_backward(place, projected, cos, sin, start, gain, query, key, value, shift, incoming):
    rows = projected.shape[0]
    return pl.pallas_call(
        backward_kernel,
        out_shape=[
            jax.ShapeDtypeStruct((rows, 256), low),
            jax.ShapeDtypeStruct((1, 256), wide),
        ],
        in_specs=[pl.BlockSpec(memory_space=pltpu.SMEM)] + in_vmem(10),
        out_specs=in_vmem(2),
        scratch_shapes=[pltpu.VMEM((rows, 128), low)] + [pltpu.VMEM((rows, 128), wide)] * 3,
        compiler_params=pltpu.CompilerParams(vmem_limit_bytes=48 * 2**20),
        cost_estimate=pl.CostEstimate(
            flops=3 * 10**9, bytes_accessed=6 * 2**20, transcendentals=2 * 10**6
        ),
        name="attention_backward",
    )(place, projected, cos, sin, start, gain, query, key, value, shift, incoming)


def adamw(weight, grad, first, second, rate, weight_decay):
    new_first = beta_one * first + (1.0 - beta_one) * grad
    new_second = beta_two * second + (1.0 - beta_two) * grad * grad
    step_size = (
        new_first
        / (1.0 - beta_one**STEP)
        / (jnp.sqrt(new_second / (1.0 - beta_two**STEP)) + adam_eps)
    )
    return (weight - rate * (step_size + weight_decay * weight), new_first, new_second)


def fold(field):
    width = field.shape[-1]
    return jnp.concatenate([field[..., i : i + 256] for i in range(0, width, 256)], axis=-2)


def unfold(field, width):
    count = width // 256
    rows = field.shape[-2] // count
    return jnp.concatenate([field[..., i * rows : (i + 1) * rows, :] for i in range(count)], axis=-1)


def pad_to(field, size, axis):
    widths = [(0, 0)] * field.ndim
    widths[axis] = (0, size - field.shape[axis])
    return jnp.pad(field, widths)


def dot(one, two):
    return jnp.dot(one, two, preferred_element_type=wide)


def dot_back(one, two):
    return jnp.einsum("tc,dc->td", one, two, preferred_element_type=wide)


def dot_rows(one, two):
    return jnp.einsum("td,tc->dc", one, two, preferred_element_type=wide)


def local(
    tokens, cotangent, lengths,
    qkv_proj, out_proj, gate_proj, down_proj, norm_gains,
    qkv_first, out_first, gate_first, down_first, gain_first,
    qkv_second, out_second, gate_second, down_second, gain_second,
):
    reps = lax.axis_size("rep")
    rows = tokens.shape[0]
    half = rows * SHARDS // 2
    own = qkv_proj.shape[0]
    block = own * SHARDS
    own_gains = norm_gains.shape[0]
    own_out = out_proj.shape[0]
    own_down = down_proj.shape[0]
    both_axes = ("rep", "shard")
    to_group = [(s * reps + r, r * SHARDS + s) for r in range(reps) for s in range(SHARDS)]
    to_owner = [(b, a) for a, b in to_group]

    token_rows = gather_rows(tokens)
    qkv_low = qkv_proj.astype(low)
    qkv_out = jnp.stack(
        [
            jnp.concatenate(
                [
                    qkv_low[:, 128 * s : 128 * s + 128],
                    qkv_low[:, QUERY_FEATURES + 64 * s : QUERY_FEATURES + 64 * s + 64],
                    qkv_low[
                        :,
                        QUERY_FEATURES + KEY_FEATURES + 64 * s : QUERY_FEATURES
                        + KEY_FEATURES
                        + 64 * s
                        + 64,
                    ],
                ],
                axis=1,
            )
            for s in range(SHARDS)
        ]
    )
    gate_low = gate_proj.astype(low)
    gate_out = jnp.stack(
        [
            jnp.concatenate(
                [
                    pad_to(gate_low[:, FF_OWN * s : FF_OWN * (s + 1)], FF_PAD, 1),
                    pad_to(gate_low[:, FF + FF_OWN * s : FF + FF_OWN * (s + 1)], FF_PAD, 1),
                ],
                axis=1,
            )
            for s in range(SHARDS)
        ]
    )
    gain_lanes = -(-own_gains // 128) * 128
    gain_out = jnp.broadcast_to(
        pad_to(pad_to(norm_gains.astype(low)[None, :], gain_lanes, 1), own, 0)[None],
        (SHARDS, own, gain_lanes),
    )
    turned = lax.all_to_all(
        jnp.concatenate([qkv_out, gate_out, gain_out], axis=2), "shard", 0, 0, tiled=True
    )
    down_pad = pad_to(down_proj.astype(low), ROWS_FF_PAD * (own_down // 36), 0)
    moved = lax.ppermute(
        jnp.concatenate([out_proj.astype(low), down_pad], axis=0), both_axes, to_group
    )
    first_parts = jnp.concatenate(
        [
            turned[:, :, :256].reshape(block, 256),
            fold(moved[:own_out]),
            pad_to(turned[:, 0, 1536:], 256, 1),
        ],
        axis=0,
    )
    second_parts = jnp.concatenate(
        [fold(turned[:, :, 256:1536].reshape(block, 2 * FF_PAD)), fold(moved[own_out:])], axis=0
    )
    first_all = lax.all_gather(first_parts, "rep", axis=0)
    second_all = lax.all_gather(second_parts, "rep", axis=0)
    qkv_w = first_all[:, :block].reshape(D, 256)
    out_w = unfold(first_all[:, block : block + 4 * own_out], D).reshape(reps * own_out, D)
    gains = first_all[:, block + 4 * own_out :, :own_gains].reshape(-1).astype(wide)
    gate_w = unfold(second_all[:, : 5 * block], 2 * FF_PAD).reshape(D, 2 * FF_PAD)
    down_w = unfold(second_all[:, 5 * block :], D)[:, :own_down].reshape(FF_OWN, D)
    down_w = pad_to(down_w, FF_PAD, 0)
    gain_attn = gains[:D]
    gain_query = gains[D : D + HEAD_SIZE]
    gain_key = gains[D + HEAD_SIZE : D + 2 * HEAD_SIZE]
    gain_ffn = gains[D + 2 * HEAD_SIZE :]
    gain_heads = jnp.concatenate([gain_query, gain_query, gain_key, gain_key])[None, :]

    shard_pos = lax.axis_index("shard")
    chip, core = shard_pos // 2, shard_pos % 2
    order = jnp.arange(SHARDS, dtype=jnp.int32)
    place = rows * (2 * ((chip + order % CHIPS) % CHIPS) + (core + order // CHIPS) % 2)
    place = place.astype(jnp.int32)
    index = jnp.arange(rows * SHARDS, dtype=jnp.int32)
    start = sequence_info(lengths[0], index)
    cos, sin = rotation_tables(index - start)
    start = start[:, None]

    inputs_all = token_rows.astype(wide)
    normed = (norm_pieces(inputs_all)[0] * gain_attn).astype(low)
    projected = dot(normed, qkv_w)
    mixed, query, key, value, shift = attention_forward(
        place, projected, cos, sin, start, gain_heads
    )
    inputs = tokens.astype(wide)
    residual = inputs + scatter_rows(dot(mixed[:half], out_w), dot(mixed[half:], out_w))
    residual_hat, residual_scale = norm_pieces(residual)
    normed_two = gather_rows((residual_hat * gain_ffn).astype(low))
    cotangent_rows = gather_rows(cotangent)
    hidden_grad = dot_back(cotangent_rows, down_w)
    both = dot(normed_two, gate_w)
    gate, upper = both[:, :FF_PAD], both[:, FF_PAD:]
    sigmoid_gate = jax.nn.sigmoid(gate)
    activated = gate * sigmoid_gate
    hidden = (activated * upper).astype(low)
    both_grad = jnp.concatenate(
        [
            hidden_grad * upper * sigmoid_gate * (1.0 + gate * (1.0 - sigmoid_gate)),
            hidden_grad * activated,
        ],
        axis=1,
    ).astype(low)

    normed_two_grad = scatter_rows(
        dot_back(both_grad[:half], gate_w), dot_back(both_grad[half:], gate_w)
    )
    gain_ffn_grad, residual_part = norm_back(
        normed_two_grad, residual_hat, residual_scale, gain_ffn
    )
    residual_grad = cotangent.astype(wide) + residual_part
    branch_grad = gather_rows(residual_grad.astype(low))
    block_output = residual + scatter_rows(dot(hidden[:half], down_w), dot(hidden[half:], down_w))
    gate_grad = dot_rows(normed_two, both_grad).astype(low)
    down_grad = dot_rows(hidden, cotangent_rows)[:FF_OWN].astype(low)
    ffn_grads = jnp.concatenate(
        [
            fold(gate_grad.reshape(reps, block, 2 * FF_PAD)),
            fold(pad_to(down_grad.reshape(reps, own_down, D), down_pad.shape[0], 1)),
        ],
        axis=1,
    )
    ffn_sums = lax.psum_scatter(
        ffn_grads.reshape(-1, 256), "rep", scatter_dimension=0, tiled=True
    )

    incoming = dot_back(branch_grad, out_w).astype(low)
    projected_grad, head_gain_grad = attention_backward(
        place, projected, cos, sin, start, gain_heads, query, key, value, shift, incoming
    )
    out_grad = dot_rows(mixed, branch_grad).astype(low)
    qkv_grad = dot_rows(normed, projected_grad).astype(low)
    last_grads = jnp.concatenate(
        [qkv_grad.reshape(reps, block, 256), fold(out_grad.reshape(reps, own_out, D))], axis=1
    )
    last_sums = jnp.sum(
        lax.all_to_all(last_grads, "rep", 0, 0, tiled=True).astype(wide), axis=0
    )
    normed_grad = scatter_rows(
        dot_back(projected_grad[:half], qkv_w), dot_back(projected_grad[half:], qkv_w)
    )
    input_hat, input_scale = norm_pieces(inputs)
    gain_attn_grad, input_part = norm_back(normed_grad, input_hat, input_scale, gain_attn)
    input_grad = residual_grad + input_part

    heads = head_gain_grad[0]
    gain_grad = jnp.concatenate(
        [
            gain_attn_grad,
            heads[:HEAD_SIZE] + heads[HEAD_SIZE : 2 * HEAD_SIZE],
            heads[2 * HEAD_SIZE : 3 * HEAD_SIZE],
            gain_ffn_grad,
        ]
    ).reshape(reps, 1, SHARDS * own_gains)
    gain_sums = jnp.sum(lax.all_to_all(gain_grad, "rep", 0, 0, tiled=True), axis=0)
    gain_back = pad_to(gain_sums.reshape(SHARDS, 1, own_gains), 256, 2)
    last_back = lax.all_to_all(
        jnp.concatenate([last_sums[:block].reshape(SHARDS, own, 256), gain_back], axis=1),
        "shard", 0, 0, tiled=True,
    )
    gain_total = jnp.sum(last_back[:, own, :own_gains], axis=0)
    qkv_total = jnp.concatenate(
        [last_back[s, :own, :128] for s in range(SHARDS)]
        + [last_back[s, :own, 128:192] for s in range(SHARDS)]
        + [last_back[s, :own, 192:] for s in range(SHARDS)],
        axis=1,
    )
    out_total = lax.ppermute(unfold(last_sums[block:], D), both_axes, to_owner)
    down_total = lax.ppermute(
        unfold(ffn_sums[5 * block :], D)[:own_down], both_axes, to_owner
    ).astype(wide)
    gate_back = lax.all_to_all(
        unfold(ffn_sums[: 5 * block], 2 * FF_PAD).reshape(SHARDS, own, 2 * FF_PAD),
        "shard", 0, 0, tiled=True,
    ).astype(wide)
    gate_total = jnp.concatenate(
        [gate_back[s, :, :FF_OWN] for s in range(SHARDS)]
        + [gate_back[s, :, FF_PAD : FF_PAD + FF_OWN] for s in range(SHARDS)],
        axis=1,
    )
    results = []
    for weight, grad, first, second, rate, weight_decay in (
        (qkv_proj, qkv_total, qkv_first, qkv_second, rate_scale * D ** (-0.5), decay),
        (out_proj, out_total, out_first, out_second, rate_scale * WO_FAN ** (-0.5), decay),
        (gate_proj, gate_total, gate_first, gate_second, rate_scale * D ** (-0.5), decay),
        (down_proj, down_total, down_first, down_second, rate_scale * FF ** (-0.5), decay),
        (norm_gains, gain_total, gain_first, gain_second, gain_rate, 0.0),
    ):
        results.extend(adamw(weight, grad, first, second, rate, weight_decay))
    return (block_output, input_grad, *results)


def solution(mesh):
    by_rows = P(("rep", "shard"), None)
    by_entry = P(("rep", "shard"))
    return jax.shard_map(
        local,
        mesh=mesh,
        in_specs=(by_rows, by_rows, P("rep", None)) + ((by_rows,) * 4 + (by_entry,)) * 3,
        out_specs=(by_rows,) * 14 + (by_entry,) * 3,
        check_vma=False,
    )
```

```python
import jax
import jax.numpy as jnp
from jax import lax
from jax.experimental import pallas as pl
from jax.experimental.pallas import tpu as pltpu
from jax.sharding import PartitionSpec as P

D = 1024
FF = 4608
HEAD_SIZE = 64
STEP = 10
QUERY_FEATURES = 1024
KEY_FEATURES = 512
WO_FAN = 4

norm_eps = 1e-05
theta = 1000000.0
beta_one = 0.9
beta_two = 0.95
adam_eps = 1e-08
decay = 0.1
rate_scale = 2.0
gain_rate = 1.0
masked_score = -1e30

SHARDS = 8
CHIPS = 4
FF_OWN = FF // SHARDS
FF_PAD = 640
ROWS_FF_PAD = 40
QUERY_BLOCK = 256
score_scale = HEAD_SIZE ** (-0.5)
low = jnp.bfloat16
wide = jnp.float32
sibling = [(i, i ^ 1) for i in range(SHARDS)]


def from_chip(k):
    return [(i, ((i // 2 - k) % CHIPS) * 2 + i % 2) for i in range(SHARDS)]


def gather_chips(rows, beside=()):
    parts = [rows] + [None] * (CHIPS - 1)
    for k in (2, 1, 3):
        parts[k] = lax.ppermute(rows, "shard", from_chip(k))
    parts[2], beside = lax.optimization_barrier((parts[2], beside))
    return jnp.concatenate(parts, axis=0), beside


def gather_rows(rows):
    mine = gather_chips(rows)[0]
    return mine, lax.ppermute(mine, "shard", sibling)


def scatter_rows(mine, other, beside=()):
    count = mine.shape[0] // CHIPS
    got = lax.ppermute(other.astype(low), "shard", sibling)
    both = mine + got.astype(wide)
    sent = both.astype(low)
    sent, beside = lax.optimization_barrier((sent, beside))
    total = both[:count]
    for k in (2, 1, 3):
        total = total + lax.ppermute(
            sent[k * count : (k + 1) * count], "shard", from_chip(-k)
        ).astype(wide)
    return total, beside


def norm_pieces(field):
    scale = lax.rsqrt(jnp.mean(field * field, axis=-1, keepdims=True) + norm_eps)
    return field * scale, scale


def norm_back(incoming_grad, normed, scale, gain):
    gain_grad = jnp.sum(incoming_grad * normed, axis=0)
    scaled = incoming_grad * gain
    inner = jnp.mean(scaled * normed, axis=-1, keepdims=True)
    return gain_grad, scale * (scaled - normed * inner)


def sequence_info(lengths_row, index):
    ends = jnp.cumsum(lengths_row)
    passed = ends[None, :] <= index[:, None]
    return jnp.sum(jnp.where(passed, lengths_row[None, :], 0), axis=1)


def rotation_tables(places):
    half = HEAD_SIZE // 2
    freqs = theta ** (-(jnp.arange(half, dtype=wide) * 2.0) / HEAD_SIZE)
    angles = places.astype(wide)[:, None] * freqs[None, :]
    cos, sin = jnp.cos(angles), jnp.sin(angles)
    return jnp.concatenate([cos] * 4, axis=1), jnp.concatenate([-sin, sin, -sin, sin], axis=1)


def lanes(rows):
    return lax.broadcasted_iota(jnp.int32, (rows, 2 * HEAD_SIZE), 1)


def partner(field):
    first = lanes(field.shape[0]) % HEAD_SIZE < HEAD_SIZE // 2
    return jnp.where(first, pltpu.roll(field, 96, 1), pltpu.roll(field, 32, 1))


def left_mean(field):
    left = lanes(field.shape[0]) < HEAD_SIZE
    return jnp.sum(jnp.where(left, field, 0.0), axis=1, keepdims=True) / HEAD_SIZE


def head_means(field):
    left = lanes(field.shape[0]) < HEAD_SIZE
    one = jnp.sum(jnp.where(left, field, 0.0), axis=1, keepdims=True) / HEAD_SIZE
    two = jnp.sum(jnp.where(left, 0.0, field), axis=1, keepdims=True) / HEAD_SIZE
    return jnp.where(left, one, two)


def swap_heads(field):
    return pltpu.roll(field, HEAD_SIZE, 1)


def stack_heads(block):
    left = (lax.broadcasted_iota(jnp.int32, (1, 2 * HEAD_SIZE), 1) < HEAD_SIZE).astype(wide)
    return jnp.concatenate([block * left.astype(low), block * (1.0 - left).astype(low)], axis=0)


def allowed_keys(start_ref, block, keys):
    begin = start_ref[block * QUERY_BLOCK : (block + 1) * QUERY_BLOCK, :]
    begin = jnp.concatenate([begin, begin], axis=0)
    row = lax.broadcasted_iota(jnp.int32, (2 * QUERY_BLOCK, keys), 0)
    row = block * QUERY_BLOCK + jnp.where(row >= QUERY_BLOCK, row - QUERY_BLOCK, row)
    col = lax.broadcasted_iota(jnp.int32, (2 * QUERY_BLOCK, keys), 1)
    return (col >= begin) & (col <= row)


def dot_last(one, two):
    return lax.dot_general(one, two, (((1,), (1,)), ((), ())), preferred_element_type=wide)


def dot_first(one, two):
    return lax.dot_general(one, two, (((0,), (0,)), ((), ())), preferred_element_type=wide)


def forward_kernel(
    place_ref, proj_ref, cos_ref, sin_ref, start_ref, gain_ref,
    out_ref, query_ref, key_ref, value_ref, shift_ref, mixed_ref,
):
    count = proj_ref.shape[0] // SHARDS
    left = lanes(count) < HEAD_SIZE
    gain_query = gain_ref[:, :128]
    gain_key = gain_ref[:, 128:]
    for chunk in range(SHARDS):
        rows = slice(chunk * count, (chunk + 1) * count)
        cos, sin = cos_ref[rows, :], sin_ref[rows, :]
        query = proj_ref[rows, :128]
        query = query * lax.rsqrt(head_means(query * query) + norm_eps) * gain_query
        query = (query * cos + partner(query) * sin).astype(low)
        query_ref[rows, :] = query * jnp.asarray(score_scale, low)
        both = proj_ref[rows, 128:]
        key = both * lax.rsqrt(left_mean(both * both) + norm_eps) * gain_key
        key = key * cos + partner(key) * sin
        both = jnp.where(left, key, both)
        turned = swap_heads(both)
        key_ref[rows, :] = jnp.where(left, both, turned).astype(low)
        value_ref[rows, :] = jnp.where(left, turned, both).astype(low)
    half = lanes(QUERY_BLOCK) < HEAD_SIZE
    for block in range(proj_ref.shape[0] // QUERY_BLOCK):
        keys = (block + 1) * QUERY_BLOCK
        span = slice(block * QUERY_BLOCK, keys)
        query = stack_heads(query_ref[span, :])
        raw = dot_last(query, key_ref[:keys, :])
        raw = jnp.where(allowed_keys(start_ref, block, keys), raw, masked_score)
        top = jnp.max(raw, axis=1, keepdims=True)
        weight = jnp.exp(raw - top)
        total = jnp.sum(weight, axis=1, keepdims=True)
        probs = (weight * (1.0 / total)).astype(low)
        mixed = jnp.dot(probs, value_ref[:keys, :], preferred_element_type=wide)
        mixed_ref[span, :] = jnp.where(half, mixed[:QUERY_BLOCK], mixed[QUERY_BLOCK:])
        shift_ref[2 * block * QUERY_BLOCK : 2 * keys, :] = top + jnp.log(total)
    for chunk in range(SHARDS):
        place = pl.multiple_of(place_ref[chunk], 128)
        out_ref[chunk] = mixed_ref[pl.ds(place, count), :].astype(low)


def backward_kernel(
    place_ref, proj_ref, cos_ref, sin_ref, start_ref, gain_ref, query_ref, key_ref, value_ref,
    shift_ref, in0_ref, in1_ref, out_ref, turned_ref, gain_grad_ref, back_ref, query_grad_ref, key_grad_ref,
    value_grad_ref,
):
    count = proj_ref.shape[0] // SHARDS
    left = lanes(count) < HEAD_SIZE
    gain_query = gain_ref[:, :128]
    gain_key = gain_ref[:, 128:]
    for chunk in range(SHARDS):
        place = pl.multiple_of(place_ref[chunk], 128)
        in_ref = (in0_ref, in1_ref)[chunk // CHIPS]
        part = slice(chunk % CHIPS * count, (chunk % CHIPS + 1) * count)
        back_ref[pl.ds(place, count), :] = in_ref[part, :]
    key_grad_ref[...] = jnp.zeros_like(key_grad_ref)
    value_grad_ref[...] = jnp.zeros_like(value_grad_ref)
    half = lanes(QUERY_BLOCK) < HEAD_SIZE
    for block in range(proj_ref.shape[0] // QUERY_BLOCK):
        keys = (block + 1) * QUERY_BLOCK
        span = slice(block * QUERY_BLOCK, keys)
        query = stack_heads(query_ref[span, :])
        back = stack_heads(back_ref[span, :])
        raw = dot_last(query, key_ref[:keys, :])
        shift = shift_ref[2 * block * QUERY_BLOCK : 2 * keys, :]
        probs = jnp.where(allowed_keys(start_ref, block, keys), jnp.exp(raw - shift), 0.0)
        prob_grad = dot_last(back, value_ref[:keys, :])
        spread = jnp.sum(probs * prob_grad, axis=1, keepdims=True)
        score_grad = (probs * (prob_grad - spread)).astype(low)
        query_grad = jnp.dot(score_grad, key_ref[:keys, :], preferred_element_type=wide)
        query_grad_ref[span, :] = score_scale * jnp.where(
            half, query_grad[:QUERY_BLOCK], query_grad[QUERY_BLOCK:]
        )
        key_grad_ref[:keys, :] += dot_first(score_grad, query)
        value_grad_ref[:keys, :] += dot_first(probs.astype(low), back)
    gain_query_grad = jnp.zeros((1, 128), wide)
    gain_key_grad = jnp.zeros((1, 128), wide)
    for chunk in range(SHARDS):
        rows = slice(chunk * count, (chunk + 1) * count)
        cos, sin = cos_ref[rows, :], sin_ref[rows, :]
        query = proj_ref[rows, :128]
        scale = lax.rsqrt(head_means(query * query) + norm_eps)
        query = query * scale
        grad = query_grad_ref[rows, :]
        grad = grad * cos - partner(grad) * sin
        gain_query_grad += jnp.sum(grad * query, axis=0, keepdims=True)
        grad = grad * gain_query
        out_ref[rows, :128] = (scale * (grad - query * head_means(grad * query))).astype(low)
        key = proj_ref[rows, 128:]
        scale = lax.rsqrt(left_mean(key * key) + norm_eps)
        key = key * scale
        grad = key_grad_ref[rows, :]
        grad = grad + swap_heads(grad)
        grad = grad * cos - partner(grad) * sin
        gain_key_grad += jnp.sum(grad * key, axis=0, keepdims=True)
        grad = grad * gain_key
        grad = scale * (grad - key * left_mean(grad * key))
        value_grad = value_grad_ref[rows, :]
        value_grad = value_grad + swap_heads(value_grad)
        out_ref[rows, 128:] = jnp.where(left, grad, value_grad).astype(low)
    for chunk in range(SHARDS):
        place = pl.multiple_of(place_ref[chunk], 128)
        turned_ref[chunk * count : (chunk + 1) * count, :] = out_ref[pl.ds(place, count), :]
    gain_grad_ref[:, :128] = gain_query_grad
    gain_grad_ref[:, 128:] = gain_key_grad


def in_vmem(count):
    return [pl.BlockSpec(memory_space=pltpu.VMEM)] * count


def attention_forward(place, projected, cos, sin, start, gain):
    rows = cos.shape[0]
    return pl.pallas_call(
        forward_kernel,
        out_shape=[jax.ShapeDtypeStruct((SHARDS, rows // SHARDS, 128), low)]
        + [jax.ShapeDtypeStruct((rows, 128), low)] * 3
        + [jax.ShapeDtypeStruct((2 * rows, 1), wide)],
        in_specs=[pl.BlockSpec(memory_space=pltpu.SMEM)] + in_vmem(5),
        out_specs=in_vmem(5),
        scratch_shapes=[pltpu.VMEM((rows, 128), wide)],
        compiler_params=pltpu.CompilerParams(vmem_limit_bytes=40 * 2**20),
        cost_estimate=pl.CostEstimate(
            flops=10**9, bytes_accessed=5 * 2**20, transcendentals=2 * 10**6
        ),
        name="attention_forward",
    )(place, projected, cos, sin, start, gain)


def attention_backward(place, projected, cos, sin, start, gain, query, key, value, shift, incoming):
    rows = cos.shape[0]
    return pl.pallas_call(
        backward_kernel,
        out_shape=[
            jax.ShapeDtypeStruct((rows, 256), low),
            jax.ShapeDtypeStruct((rows, 256), low),
            jax.ShapeDtypeStruct((1, 256), wide),
        ],
        in_specs=[pl.BlockSpec(memory_space=pltpu.SMEM)] + in_vmem(11),
        out_specs=in_vmem(3),
        scratch_shapes=[pltpu.VMEM((rows, 128), low)] + [pltpu.VMEM((rows, 128), wide)] * 3,
        compiler_params=pltpu.CompilerParams(vmem_limit_bytes=48 * 2**20),
        cost_estimate=pl.CostEstimate(
            flops=3 * 10**9, bytes_accessed=6 * 2**20, transcendentals=2 * 10**6
        ),
        name="attention_backward",
    )(place, projected, cos, sin, start, gain, query, key, value, shift, *incoming)


def copy_kernel(order_ref, in_ref, out_ref):
    out_ref[...] = in_ref[...]


def reorder(order, field, rows):
    width = field.shape[1]
    return pl.pallas_call(
        copy_kernel,
        grid_spec=pltpu.PrefetchScalarGridSpec(
            num_scalar_prefetch=1,
            grid=(SHARDS,),
            in_specs=[pl.BlockSpec((rows, width), lambda i, order: (order[i], 0))],
            out_specs=pl.BlockSpec((rows, width), lambda i, order: (i, 0)),
        ),
        out_shape=jax.ShapeDtypeStruct((SHARDS * rows, width), field.dtype),
        cost_estimate=pl.CostEstimate(flops=0, bytes_accessed=4 * 2**20, transcendentals=0),
        name="reorder",
    )(order, field)


def adamw(weight, grad, first, second, rate, weight_decay):
    new_first = beta_one * first + (1.0 - beta_one) * grad
    new_second = beta_two * second + (1.0 - beta_two) * grad * grad
    step_size = (
        new_first
        / (1.0 - beta_one**STEP)
        / (jnp.sqrt(new_second / (1.0 - beta_two**STEP)) + adam_eps)
    )
    return (weight - rate * (step_size + weight_decay * weight), new_first, new_second)


def fold(field):
    width = field.shape[-1]
    return jnp.concatenate([field[..., i : i + 256] for i in range(0, width, 256)], axis=-2)


def unfold(field, width):
    count = width // 256
    rows = field.shape[-2] // count
    return jnp.concatenate([field[..., i * rows : (i + 1) * rows, :] for i in range(count)], axis=-1)


def pad_to(field, size, axis):
    widths = [(0, 0)] * field.ndim
    widths[axis] = (0, size - field.shape[axis])
    return jnp.pad(field, widths)


def dot(one, two):
    return jnp.dot(one, two, preferred_element_type=wide)


def dot_back(one, two):
    return jnp.einsum("tc,dc->td", one, two, preferred_element_type=wide)


def dot_rows(one, two):
    return jnp.einsum("td,tc->dc", one, two, preferred_element_type=wide)


def local(
    tokens, cotangent, lengths,
    qkv_proj, out_proj, gate_proj, down_proj, norm_gains,
    qkv_first, out_first, gate_first, down_first, gain_first,
    qkv_second, out_second, gate_second, down_second, gain_second,
):
    reps = lax.axis_size("rep")
    rows = tokens.shape[0]
    half = rows * SHARDS // 2
    own = qkv_proj.shape[0]
    block = own * SHARDS
    own_gains = norm_gains.shape[0]
    own_out = out_proj.shape[0]
    own_down = down_proj.shape[0]
    both_axes = ("rep", "shard")
    to_group = [(s * reps + r, r * SHARDS + s) for r in range(reps) for s in range(SHARDS)]
    to_owner = [(b, a) for a, b in to_group]

    qkv_low = qkv_proj.astype(low)
    qkv_out = jnp.stack(
        [
            jnp.concatenate(
                [
                    qkv_low[:, 128 * s : 128 * s + 128],
                    qkv_low[:, QUERY_FEATURES + 64 * s : QUERY_FEATURES + 64 * s + 64],
                    qkv_low[
                        :,
                        QUERY_FEATURES + KEY_FEATURES + 64 * s : QUERY_FEATURES
                        + KEY_FEATURES
                        + 64 * s
                        + 64,
                    ],
                ],
                axis=1,
            )
            for s in range(SHARDS)
        ]
    )
    gate_low = gate_proj.astype(low)
    gate_out = jnp.stack(
        [
            jnp.concatenate(
                [
                    pad_to(gate_low[:, FF_OWN * s : FF_OWN * (s + 1)], FF_PAD, 1),
                    pad_to(gate_low[:, FF + FF_OWN * s : FF + FF_OWN * (s + 1)], FF_PAD, 1),
                ],
                axis=1,
            )
            for s in range(SHARDS)
        ]
    )
    gain_lanes = -(-own_gains // 128) * 128
    gain_out = jnp.broadcast_to(
        pad_to(pad_to(norm_gains.astype(low)[None, :], gain_lanes, 1), own, 0)[None],
        (SHARDS, own, gain_lanes),
    )
    turned = jnp.concatenate([qkv_out, gate_out, gain_out], axis=2)
    turned = lax.all_to_all(turned, "shard", 0, 0, tiled=True)
    both_rows = lax.all_gather(
        jnp.concatenate([tokens, cotangent], axis=0), "shard", axis=0, tiled=True
    )
    token_rows = both_rows.reshape(SHARDS, 2, rows, D)[:, 0].reshape(2 * half, D)
    down_pad = pad_to(down_proj.astype(low), ROWS_FF_PAD * (own_down // 36), 0)
    moved = lax.ppermute(
        jnp.concatenate([out_proj.astype(low), down_pad], axis=0), both_axes, to_group
    )
    first_parts = jnp.concatenate(
        [
            turned[:, :, :256].reshape(block, 256),
            fold(moved[:own_out]),
            pad_to(turned[:, 0, 1536:], 256, 1),
        ],
        axis=0,
    )
    second_parts = jnp.concatenate(
        [
            turned[:, :, 256:1536].reshape(block, 2 * FF_PAD),
            pad_to(moved[own_out:], 2 * FF_PAD, 1),
        ],
        axis=0,
    )
    second_all = lax.all_gather(second_parts, "rep", axis=0)
    first_all = lax.all_gather(first_parts, "rep", axis=0)
    qkv_w = first_all[:, :block].reshape(D, 256)
    out_w = unfold(first_all[:, block : block + 4 * own_out], D).reshape(reps * own_out, D)
    gains = first_all[:, block + 4 * own_out :, :own_gains].reshape(-1).astype(wide)
    gain_attn = gains[:D]
    gain_query = gains[D : D + HEAD_SIZE]
    gain_key = gains[D + HEAD_SIZE : D + 2 * HEAD_SIZE]
    gain_ffn = gains[D + 2 * HEAD_SIZE :]
    gain_heads = jnp.concatenate([gain_query, gain_query, gain_key, gain_key])[None, :]

    shard_pos = lax.axis_index("shard")
    chip, core = shard_pos // 2, shard_pos % 2
    order = jnp.arange(SHARDS, dtype=jnp.int32)
    place = rows * (2 * ((chip + order % CHIPS) % CHIPS) + (core + order // CHIPS) % 2)
    place = place.astype(jnp.int32)
    index = jnp.arange(rows * SHARDS, dtype=jnp.int32)
    start = sequence_info(lengths[0], index)
    cos, sin = rotation_tables(index - start)
    start = start[:, None]

    inputs_hat = norm_pieces(token_rows.astype(wide))[0]
    normed = (inputs_hat * gain_attn).astype(low)
    projected = dot(normed, qkv_w)
    cotangent_rows = reorder(2 * place // rows + 1, both_rows, rows)
    cotangent_rows = cotangent_rows[:half], cotangent_rows[half:]
    mixed, query, key, value, shift = attention_forward(
        place, projected, cos, sin, start, gain_heads
    )
    mixed = mixed[:CHIPS].reshape(half, 128), mixed[CHIPS:].reshape(half, 128)
    inputs = tokens.astype(wide)
    residual = inputs + scatter_rows(*[dot(part, out_w) for part in mixed])[0]
    residual, second_all = lax.optimization_barrier((residual, second_all))
    gate_w = second_all[:, :block].reshape(D, 2 * FF_PAD)
    down_w = pad_to(second_all[:, block : block + own_down, :D].reshape(FF_OWN, D), FF_PAD, 0)
    residual_hat, residual_scale = norm_pieces(residual)
    hidden_grads = [dot_back(part, down_w) for part in cotangent_rows]
    mine, (gate_w, hidden_grads) = gather_chips(
        (residual_hat * gain_ffn).astype(low), (gate_w, hidden_grads)
    )
    normed_two = mine, lax.ppermute(mine, "shard", sibling)
    hidden, both_grad = [], []
    for j in range(2):
        hidden_grad = hidden_grads[j]
        both = dot(normed_two[j], gate_w)
        gate, upper = both[:, :FF_PAD], both[:, FF_PAD:]
        sigmoid_gate = jax.nn.sigmoid(gate)
        activated = gate * sigmoid_gate
        hidden.append((activated * upper).astype(low))
        both_grad.append(
            jnp.concatenate(
                [
                    hidden_grad * upper * sigmoid_gate * (1.0 + gate * (1.0 - sigmoid_gate)),
                    hidden_grad * activated,
                ],
                axis=1,
            ).astype(low)
        )

    normed_two_grad, (hidden, both_grad) = scatter_rows(
        dot_back(both_grad[0], gate_w), dot_back(both_grad[1], gate_w), (hidden, both_grad)
    )
    gate_grad = sum(map(dot_rows, normed_two, both_grad)).astype(low)
    down_grad = sum(map(dot_rows, hidden, cotangent_rows))[:FF_OWN].astype(low)
    down_grad = down_grad.reshape(reps, own_down, D)
    ffn_grads = jnp.concatenate(
        [
            gate_grad.reshape(reps, block, 2 * FF_PAD),
            jnp.pad(
                down_grad, ((0, 0), (0, down_pad.shape[0] - own_down), (0, 2 * FF_PAD - D))
            ),
        ],
        axis=1,
    )
    normed_two_grad, ffn_grads = lax.optimization_barrier((normed_two_grad, ffn_grads))
    ffn_sums = lax.psum_scatter(
        ffn_grads.reshape(-1, 2 * FF_PAD), "rep", scatter_dimension=0, tiled=True
    )
    gain_ffn_grad, residual_part = norm_back(
        normed_two_grad, residual_hat, residual_scale, gain_ffn
    )
    residual_grad = cotangent.astype(wide) + residual_part
    branch_own = residual_grad.astype(low)
    branch_grad = gather_rows(branch_own)
    incoming = [dot_back(part, out_w).astype(low) for part in branch_grad]
    projected_grad, turned_grad, head_gain_grad = attention_backward(
        place, projected, cos, sin, start, gain_heads, query, key, value, shift, incoming
    )
    normed_parts = [dot_back(part, qkv_w) for part in (turned_grad[:half], turned_grad[half:])]
    gain_attn_grad = jnp.sum(dot_back(projected_grad, qkv_w) * inputs_hat, axis=0)
    out_grad = sum(map(dot_rows, mixed, branch_grad)).astype(low)
    qkv_grad = dot_rows(normed, projected_grad).astype(low)
    heads = head_gain_grad[0]
    gain_grad = jnp.concatenate(
        [
            gain_attn_grad,
            heads[:HEAD_SIZE] + heads[HEAD_SIZE : 2 * HEAD_SIZE],
            heads[2 * HEAD_SIZE : 3 * HEAD_SIZE],
            gain_ffn_grad,
        ]
    ).astype(low)
    gain_grad = pad_to(gain_grad.reshape(reps, SHARDS, own_gains), 256, 2)
    last_grads = jnp.concatenate(
        [
            qkv_grad.reshape(reps, block, 256),
            fold(out_grad.reshape(reps, own_out, D)),
            gain_grad,
        ],
        axis=1,
    )
    last_grads, normed_parts = lax.optimization_barrier((last_grads, normed_parts))
    normed_grad, hidden = scatter_rows(*normed_parts, hidden)
    input_hat, input_scale = norm_pieces(inputs)
    input_part = norm_back(normed_grad, input_hat, input_scale, gain_attn)[1]
    input_grad = residual_grad + input_part
    block_output = residual + scatter_rows(*[dot(part, down_w) for part in hidden])[0]
    last_sums = jnp.sum(
        lax.all_to_all(last_grads, "rep", 0, 0, tiled=True).astype(wide), axis=0
    )
    last_sums, input_grad, block_output, ffn_sums = lax.optimization_barrier(
        (last_sums, input_grad, block_output, ffn_sums)
    )
    ffn_sums = ffn_sums.astype(wide)
    gate_sums, down_sums = ffn_sums[:block], ffn_sums[block:, :D]
    back = lax.all_to_all(
        jnp.concatenate(
            [
                jnp.concatenate(
                    [
                        last_sums[:block].reshape(SHARDS, own, 256),
                        gate_sums.reshape(SHARDS, own, 2 * FF_PAD),
                    ],
                    axis=2,
                ),
                pad_to(
                    last_sums[block + 4 * own_out :].reshape(SHARDS, 1, 256), 256 + 2 * FF_PAD, 2
                ),
            ],
            axis=1,
        ).astype(low),
        "shard", 0, 0, tiled=True,
    ).astype(wide)
    last_back, gate_back = back[:, :, :256], back[:, :own, 256:]
    gain_total = jnp.sum(last_back[:, own, :own_gains], axis=0)
    qkv_total = jnp.concatenate(
        [last_back[s, :own, :128] for s in range(SHARDS)]
        + [last_back[s, :own, 128:192] for s in range(SHARDS)]
        + [last_back[s, :own, 192:] for s in range(SHARDS)],
        axis=1,
    )
    back = lax.ppermute(
        jnp.concatenate(
            [
                unfold(last_sums[block : block + 4 * own_out], D),
                down_sums,
            ],
            axis=0,
        ),
        both_axes,
        to_owner,
    )
    out_total, down_total = back[:own_out], back[own_out : own_out + own_down]
    gate_total = jnp.concatenate(
        [gate_back[s, :, :FF_OWN] for s in range(SHARDS)]
        + [gate_back[s, :, FF_PAD : FF_PAD + FF_OWN] for s in range(SHARDS)],
        axis=1,
    )
    results = []
    for weight, grad, first, second, rate, weight_decay in (
        (qkv_proj, qkv_total, qkv_first, qkv_second, rate_scale * D ** (-0.5), decay),
        (out_proj, out_total, out_first, out_second, rate_scale * WO_FAN ** (-0.5), decay),
        (gate_proj, gate_total, gate_first, gate_second, rate_scale * D ** (-0.5), decay),
        (down_proj, down_total, down_first, down_second, rate_scale * FF ** (-0.5), decay),
        (norm_gains, gain_total, gain_first, gain_second, gain_rate, 0.0),
    ):
        results.extend(adamw(weight, grad, first, second, rate, weight_decay))
    return (block_output, input_grad, *results)


def solution(mesh):
    by_rows = P(("rep", "shard"), None)
    by_entry = P(("rep", "shard"))
    return jax.shard_map(
        local,
        mesh=mesh,
        in_specs=(by_rows, by_rows, P("rep", None)) + ((by_rows,) * 4 + (by_entry,)) * 3,
        out_specs=(by_rows,) * 14 + (by_entry,) * 3,
        check_vma=False,
    )
```

```python
import jax
import jax.numpy as jnp
from jax import lax
from jax.experimental import pallas as pl
from jax.experimental.pallas import tpu as pltpu
from jax.sharding import PartitionSpec as P

D = 1024
FF = 4608
HEAD_SIZE = 64
STEP = 10
QUERY_FEATURES = 1024
KEY_FEATURES = 512
WO_FAN = 4

norm_eps = 1e-05
theta = 1000000.0
beta_one = 0.9
beta_two = 0.95
adam_eps = 1e-08
decay = 0.1
rate_scale = 2.0
gain_rate = 1.0
masked_score = -1e30

SHARDS = 8
CHIPS = 4
FF_OWN = FF // SHARDS
FF_PAD = 640
ROWS_FF_PAD = 40
QUERY_BLOCK = 256
score_scale = HEAD_SIZE ** (-0.5)
low = jnp.bfloat16
wide = jnp.float32
sibling = [(i, i ^ 1) for i in range(SHARDS)]


def from_chip(k):
    return [(i, ((i // 2 - k) % CHIPS) * 2 + i % 2) for i in range(SHARDS)]


def gather_chips(rows, beside=()):
    parts = [rows] + [None] * (CHIPS - 1)
    for k in (2, 1, 3):
        parts[k] = lax.ppermute(rows, "shard", from_chip(k))
    parts[2], beside = lax.optimization_barrier((parts[2], beside))
    return jnp.concatenate(parts, axis=0), beside


def gather_rows(rows):
    mine = gather_chips(rows)[0]
    return mine, lax.ppermute(mine, "shard", sibling)


def scatter_rows(mine, other, beside=()):
    count = mine.shape[0] // CHIPS
    got = lax.ppermute(other.astype(low), "shard", sibling)
    both = mine + got.astype(wide)
    sent = both.astype(low)
    sent, beside = lax.optimization_barrier((sent, beside))
    total = both[:count]
    for k in (2, 1, 3):
        total = total + lax.ppermute(
            sent[k * count : (k + 1) * count], "shard", from_chip(-k)
        ).astype(wide)
    return total, beside


def norm_pieces(field):
    scale = lax.rsqrt(jnp.mean(field * field, axis=-1, keepdims=True) + norm_eps)
    return field * scale, scale


def norm_back(incoming_grad, normed, scale, gain):
    gain_grad = jnp.sum(incoming_grad * normed, axis=0)
    scaled = incoming_grad * gain
    inner = jnp.mean(scaled * normed, axis=-1, keepdims=True)
    return gain_grad, scale * (scaled - normed * inner)


def sequence_info(lengths_row, index):
    ends = jnp.cumsum(lengths_row)
    passed = ends[None, :] <= index[:, None]
    return jnp.sum(jnp.where(passed, lengths_row[None, :], 0), axis=1)


def rotation_tables(places):
    half = HEAD_SIZE // 2
    freqs = theta ** (-(jnp.arange(half, dtype=wide) * 2.0) / HEAD_SIZE)
    angles = places.astype(wide)[:, None] * freqs[None, :]
    cos, sin = jnp.cos(angles), jnp.sin(angles)
    return jnp.concatenate([cos] * 4, axis=1), jnp.concatenate([-sin, sin, -sin, sin], axis=1)


def lanes(rows):
    return lax.broadcasted_iota(jnp.int32, (rows, 2 * HEAD_SIZE), 1)


def partner(field):
    first = lanes(field.shape[0]) % HEAD_SIZE < HEAD_SIZE // 2
    return jnp.where(first, pltpu.roll(field, 96, 1), pltpu.roll(field, 32, 1))


def left_mean(field):
    left = lanes(field.shape[0]) < HEAD_SIZE
    return jnp.sum(jnp.where(left, field, 0.0), axis=1, keepdims=True) / HEAD_SIZE


def head_means(field):
    left = lanes(field.shape[0]) < HEAD_SIZE
    one = jnp.sum(jnp.where(left, field, 0.0), axis=1, keepdims=True) / HEAD_SIZE
    two = jnp.sum(jnp.where(left, 0.0, field), axis=1, keepdims=True) / HEAD_SIZE
    return jnp.where(left, one, two)


def swap_heads(field):
    return pltpu.roll(field, HEAD_SIZE, 1)


def stack_heads(block):
    left = (lax.broadcasted_iota(jnp.int32, (1, 2 * HEAD_SIZE), 1) < HEAD_SIZE).astype(wide)
    return jnp.concatenate([block * left.astype(low), block * (1.0 - left).astype(low)], axis=0)


def allowed_keys(start_ref, block, keys):
    begin = start_ref[block * QUERY_BLOCK : (block + 1) * QUERY_BLOCK, :]
    begin = jnp.concatenate([begin, begin], axis=0)
    row = lax.broadcasted_iota(jnp.int32, (2 * QUERY_BLOCK, keys), 0)
    row = block * QUERY_BLOCK + jnp.where(row >= QUERY_BLOCK, row - QUERY_BLOCK, row)
    col = lax.broadcasted_iota(jnp.int32, (2 * QUERY_BLOCK, keys), 1)
    return (col >= begin) & (col <= row)


def dot_last(one, two):
    return lax.dot_general(one, two, (((1,), (1,)), ((), ())), preferred_element_type=wide)


def dot_first(one, two):
    return lax.dot_general(one, two, (((0,), (0,)), ((), ())), preferred_element_type=wide)


def forward_kernel(
    place_ref, proj_ref, cos_ref, sin_ref, start_ref, gain_ref,
    out_ref, query_ref, key_ref, value_ref, shift_ref, mixed_ref,
):
    count = proj_ref.shape[0] // SHARDS
    left = lanes(count) < HEAD_SIZE
    gain_query = gain_ref[:, :128]
    gain_key = gain_ref[:, 128:]
    for chunk in range(SHARDS):
        rows = slice(chunk * count, (chunk + 1) * count)
        cos, sin = cos_ref[rows, :], sin_ref[rows, :]
        query = proj_ref[rows, :128]
        query = query * lax.rsqrt(head_means(query * query) + norm_eps) * gain_query
        query = (query * cos + partner(query) * sin).astype(low)
        query_ref[rows, :] = query * jnp.asarray(score_scale, low)
        both = proj_ref[rows, 128:]
        key = both * lax.rsqrt(left_mean(both * both) + norm_eps) * gain_key
        key = key * cos + partner(key) * sin
        both = jnp.where(left, key, both)
        turned = swap_heads(both)
        key_ref[rows, :] = jnp.where(left, both, turned).astype(low)
        value_ref[rows, :] = jnp.where(left, turned, both).astype(low)
    half = lanes(QUERY_BLOCK) < HEAD_SIZE
    for block in range(proj_ref.shape[0] // QUERY_BLOCK):
        keys = (block + 1) * QUERY_BLOCK
        span = slice(block * QUERY_BLOCK, keys)
        query = stack_heads(query_ref[span, :])
        raw = dot_last(query, key_ref[:keys, :])
        raw = jnp.where(allowed_keys(start_ref, block, keys), raw, masked_score)
        top = jnp.max(raw, axis=1, keepdims=True)
        weight = jnp.exp(raw - top)
        total = jnp.sum(weight, axis=1, keepdims=True)
        probs = (weight * (1.0 / total)).astype(low)
        mixed = jnp.dot(probs, value_ref[:keys, :], preferred_element_type=wide)
        mixed_ref[span, :] = jnp.where(half, mixed[:QUERY_BLOCK], mixed[QUERY_BLOCK:])
        shift_ref[2 * block * QUERY_BLOCK : 2 * keys, :] = top + jnp.log(total)
    for chunk in range(SHARDS):
        place = pl.multiple_of(place_ref[chunk], 128)
        out_ref[chunk] = mixed_ref[pl.ds(place, count), :].astype(low)


def backward_kernel(
    place_ref, proj_ref, cos_ref, sin_ref, start_ref, gain_ref, query_ref, key_ref, value_ref,
    shift_ref, in0_ref, in1_ref, out_ref, turned_ref, gain_grad_ref, back_ref, query_grad_ref, key_grad_ref,
    value_grad_ref,
):
    count = proj_ref.shape[0] // SHARDS
    left = lanes(count) < HEAD_SIZE
    gain_query = gain_ref[:, :128]
    gain_key = gain_ref[:, 128:]
    for chunk in range(SHARDS):
        place = pl.multiple_of(place_ref[chunk], 128)
        in_ref = (in0_ref, in1_ref)[chunk // CHIPS]
        part = slice(chunk % CHIPS * count, (chunk % CHIPS + 1) * count)
        back_ref[pl.ds(place, count), :] = in_ref[part, :]
    key_grad_ref[...] = jnp.zeros_like(key_grad_ref)
    value_grad_ref[...] = jnp.zeros_like(value_grad_ref)
    half = lanes(QUERY_BLOCK) < HEAD_SIZE
    for block in range(proj_ref.shape[0] // QUERY_BLOCK):
        keys = (block + 1) * QUERY_BLOCK
        span = slice(block * QUERY_BLOCK, keys)
        query = stack_heads(query_ref[span, :])
        back = stack_heads(back_ref[span, :])
        raw = dot_last(query, key_ref[:keys, :])
        shift = shift_ref[2 * block * QUERY_BLOCK : 2 * keys, :]
        probs = jnp.where(allowed_keys(start_ref, block, keys), jnp.exp(raw - shift), 0.0)
        prob_grad = dot_last(back, value_ref[:keys, :])
        spread = jnp.sum(probs * prob_grad, axis=1, keepdims=True)
        score_grad = (probs * (prob_grad - spread)).astype(low)
        query_grad = jnp.dot(score_grad, key_ref[:keys, :], preferred_element_type=wide)
        query_grad_ref[span, :] = score_scale * jnp.where(
            half, query_grad[:QUERY_BLOCK], query_grad[QUERY_BLOCK:]
        )
        key_grad_ref[:keys, :] += dot_first(score_grad, query)
        value_grad_ref[:keys, :] += dot_first(probs.astype(low), back)
    gain_query_grad = jnp.zeros((1, 128), wide)
    gain_key_grad = jnp.zeros((1, 128), wide)
    for chunk in range(SHARDS):
        rows = slice(chunk * count, (chunk + 1) * count)
        cos, sin = cos_ref[rows, :], sin_ref[rows, :]
        query = proj_ref[rows, :128]
        scale = lax.rsqrt(head_means(query * query) + norm_eps)
        query = query * scale
        grad = query_grad_ref[rows, :]
        grad = grad * cos - partner(grad) * sin
        gain_query_grad += jnp.sum(grad * query, axis=0, keepdims=True)
        grad = grad * gain_query
        out_ref[rows, :128] = (scale * (grad - query * head_means(grad * query))).astype(low)
        key = proj_ref[rows, 128:]
        scale = lax.rsqrt(left_mean(key * key) + norm_eps)
        key = key * scale
        grad = key_grad_ref[rows, :]
        grad = grad + swap_heads(grad)
        grad = grad * cos - partner(grad) * sin
        gain_key_grad += jnp.sum(grad * key, axis=0, keepdims=True)
        grad = grad * gain_key
        grad = scale * (grad - key * left_mean(grad * key))
        value_grad = value_grad_ref[rows, :]
        value_grad = value_grad + swap_heads(value_grad)
        out_ref[rows, 128:] = jnp.where(left, grad, value_grad).astype(low)
    for chunk in range(SHARDS):
        place = pl.multiple_of(place_ref[chunk], 128)
        turned_ref[chunk * count : (chunk + 1) * count, :] = out_ref[pl.ds(place, count), :]
    gain_grad_ref[:, :128] = gain_query_grad
    gain_grad_ref[:, 128:] = gain_key_grad


def in_vmem(count):
    return [pl.BlockSpec(memory_space=pltpu.VMEM)] * count


def attention_forward(place, projected, cos, sin, start, gain):
    rows = cos.shape[0]
    return pl.pallas_call(
        forward_kernel,
        out_shape=[jax.ShapeDtypeStruct((SHARDS, rows // SHARDS, 128), low)]
        + [jax.ShapeDtypeStruct((rows, 128), low)] * 3
        + [jax.ShapeDtypeStruct((2 * rows, 1), wide)],
        in_specs=[pl.BlockSpec(memory_space=pltpu.SMEM)] + in_vmem(5),
        out_specs=in_vmem(5),
        scratch_shapes=[pltpu.VMEM((rows, 128), wide)],
        compiler_params=pltpu.CompilerParams(vmem_limit_bytes=40 * 2**20),
        cost_estimate=pl.CostEstimate(
            flops=10**9, bytes_accessed=5 * 2**20, transcendentals=2 * 10**6
        ),
        name="attention_forward",
    )(place, projected, cos, sin, start, gain)


def attention_backward(place, projected, cos, sin, start, gain, query, key, value, shift, incoming):
    rows = cos.shape[0]
    return pl.pallas_call(
        backward_kernel,
        out_shape=[
            jax.ShapeDtypeStruct((rows, 256), low),
            jax.ShapeDtypeStruct((rows, 256), low),
            jax.ShapeDtypeStruct((1, 256), wide),
        ],
        in_specs=[pl.BlockSpec(memory_space=pltpu.SMEM)] + in_vmem(11),
        out_specs=in_vmem(3),
        scratch_shapes=[pltpu.VMEM((rows, 128), low)] + [pltpu.VMEM((rows, 128), wide)] * 3,
        compiler_params=pltpu.CompilerParams(vmem_limit_bytes=48 * 2**20),
        cost_estimate=pl.CostEstimate(
            flops=3 * 10**9, bytes_accessed=6 * 2**20, transcendentals=2 * 10**6
        ),
        name="attention_backward",
    )(place, projected, cos, sin, start, gain, query, key, value, shift, *incoming)


def copy_kernel(order_ref, in_ref, out_ref):
    out_ref[...] = in_ref[...]


def reorder(order, field, rows):
    width = field.shape[1]
    return pl.pallas_call(
        copy_kernel,
        grid_spec=pltpu.PrefetchScalarGridSpec(
            num_scalar_prefetch=1,
            grid=(SHARDS,),
            in_specs=[pl.BlockSpec((rows, width), lambda i, order: (order[i], 0))],
            out_specs=pl.BlockSpec((rows, width), lambda i, order: (i, 0)),
        ),
        out_shape=jax.ShapeDtypeStruct((SHARDS * rows, width), field.dtype),
        cost_estimate=pl.CostEstimate(flops=0, bytes_accessed=4 * 2**20, transcendentals=0),
        name="reorder",
    )(order, field)


def adamw(weight, grad, first, second, rate, weight_decay):
    new_first = beta_one * first + (1.0 - beta_one) * grad
    new_second = beta_two * second + (1.0 - beta_two) * grad * grad
    step_size = (
        new_first
        / (1.0 - beta_one**STEP)
        / (jnp.sqrt(new_second / (1.0 - beta_two**STEP)) + adam_eps)
    )
    return (weight - rate * (step_size + weight_decay * weight), new_first, new_second)


def fold(field):
    width = field.shape[-1]
    return jnp.concatenate([field[..., i : i + 256] for i in range(0, width, 256)], axis=-2)


def unfold(field, width):
    count = width // 256
    rows = field.shape[-2] // count
    return jnp.concatenate([field[..., i * rows : (i + 1) * rows, :] for i in range(count)], axis=-1)


def rep_groups(reps):
    side = 4 if reps == 16 else 1
    count = reps // side
    return (
        [[side * x + y for x in range(count)] for y in range(side)],
        [[side * x + y for y in range(side)] for x in range(count)],
    )


def pad_to(field, size, axis):
    widths = [(0, 0)] * field.ndim
    widths[axis] = (0, size - field.shape[axis])
    return jnp.pad(field, widths)


def dot(one, two):
    return jnp.dot(one, two, preferred_element_type=wide)


def dot_back(one, two):
    return jnp.einsum("tc,dc->td", one, two, preferred_element_type=wide)


def dot_rows(one, two):
    return jnp.einsum("td,tc->dc", one, two, preferred_element_type=wide)


def local(
    tokens, cotangent, lengths,
    qkv_proj, out_proj, gate_proj, down_proj, norm_gains,
    qkv_first, out_first, gate_first, down_first, gain_first,
    qkv_second, out_second, gate_second, down_second, gain_second,
):
    reps = lax.axis_size("rep")
    rows = tokens.shape[0]
    half = rows * SHARDS // 2
    own = qkv_proj.shape[0]
    block = own * SHARDS
    own_gains = norm_gains.shape[0]
    own_out = out_proj.shape[0]
    own_down = down_proj.shape[0]
    both_axes = ("rep", "shard")
    to_group = [(s * reps + r, r * SHARDS + s) for r in range(reps) for s in range(SHARDS)]
    to_owner = [(b, a) for a, b in to_group]

    qkv_low = qkv_proj.astype(low)
    qkv_out = jnp.stack(
        [
            jnp.concatenate(
                [
                    qkv_low[:, 128 * s : 128 * s + 128],
                    qkv_low[:, QUERY_FEATURES + 64 * s : QUERY_FEATURES + 64 * s + 64],
                    qkv_low[
                        :,
                        QUERY_FEATURES + KEY_FEATURES + 64 * s : QUERY_FEATURES
                        + KEY_FEATURES
                        + 64 * s
                        + 64,
                    ],
                ],
                axis=1,
            )
            for s in range(SHARDS)
        ]
    )
    gate_low = gate_proj.astype(low)
    gate_out = jnp.stack(
        [
            jnp.concatenate(
                [
                    pad_to(gate_low[:, FF_OWN * s : FF_OWN * (s + 1)], FF_PAD, 1),
                    pad_to(gate_low[:, FF + FF_OWN * s : FF + FF_OWN * (s + 1)], FF_PAD, 1),
                ],
                axis=1,
            )
            for s in range(SHARDS)
        ]
    )
    gain_lanes = -(-own_gains // 128) * 128
    gain_out = jnp.broadcast_to(
        pad_to(pad_to(norm_gains.astype(low)[None, :], gain_lanes, 1), own, 0)[None],
        (SHARDS, own, gain_lanes),
    )
    turned = jnp.concatenate([qkv_out, gate_out, gain_out], axis=2)
    turned = lax.all_to_all(turned, "shard", 0, 0, tiled=True)
    both_rows = lax.all_gather(
        jnp.concatenate([tokens, cotangent], axis=0), "shard", axis=0, tiled=True
    )
    token_rows = both_rows.reshape(SHARDS, 2, rows, D)[:, 0].reshape(2 * half, D)
    down_pad = pad_to(down_proj.astype(low), ROWS_FF_PAD * (own_down // 36), 0)
    moved = lax.ppermute(
        jnp.concatenate([out_proj.astype(low), down_pad], axis=0), both_axes, to_group
    )
    first_parts = jnp.concatenate(
        [
            turned[:, :, :256].reshape(block, 256),
            fold(moved[:own_out]),
            pad_to(turned[:, 0, 1536:], 256, 1),
        ],
        axis=0,
    )
    second_parts = jnp.concatenate(
        [
            turned[:, :, 256:1536].reshape(block, 2 * FF_PAD),
            pad_to(moved[own_out:], 2 * FF_PAD, 1),
        ],
        axis=0,
    )
    second_all = lax.all_gather(second_parts, "rep", axis=0)
    first_all = lax.all_gather(first_parts, "rep", axis=0)
    qkv_w = first_all[:, :block].reshape(D, 256)
    out_w = unfold(first_all[:, block : block + 4 * own_out], D).reshape(reps * own_out, D)
    gains = first_all[:, block + 4 * own_out :, :own_gains].reshape(-1).astype(wide)
    gain_attn = gains[:D]
    gain_query = gains[D : D + HEAD_SIZE]
    gain_key = gains[D + HEAD_SIZE : D + 2 * HEAD_SIZE]
    gain_ffn = gains[D + 2 * HEAD_SIZE :]
    gain_heads = jnp.concatenate([gain_query, gain_query, gain_key, gain_key])[None, :]

    shard_pos = lax.axis_index("shard")
    chip, core = shard_pos // 2, shard_pos % 2
    order = jnp.arange(SHARDS, dtype=jnp.int32)
    place = rows * (2 * ((chip + order % CHIPS) % CHIPS) + (core + order // CHIPS) % 2)
    place = place.astype(jnp.int32)
    index = jnp.arange(rows * SHARDS, dtype=jnp.int32)
    start = sequence_info(lengths[0], index)
    cos, sin = rotation_tables(index - start)
    start = start[:, None]

    inputs_hat = norm_pieces(token_rows.astype(wide))[0]
    normed = (inputs_hat * gain_attn).astype(low)
    projected = dot(normed, qkv_w)
    cotangent_rows = reorder(2 * place // rows + 1, both_rows, rows)
    cotangent_rows = cotangent_rows[:half], cotangent_rows[half:]
    mixed, query, key, value, shift = attention_forward(
        place, projected, cos, sin, start, gain_heads
    )
    mixed = mixed[:CHIPS].reshape(half, 128), mixed[CHIPS:].reshape(half, 128)
    inputs = tokens.astype(wide)
    residual = inputs + scatter_rows(*[dot(part, out_w) for part in mixed])[0]
    residual, second_all = lax.optimization_barrier((residual, second_all))
    gate_w = second_all[:, :block].reshape(D, 2 * FF_PAD)
    down_w = pad_to(second_all[:, block : block + own_down, :D].reshape(FF_OWN, D), FF_PAD, 0)
    residual_hat, residual_scale = norm_pieces(residual)
    hidden_grads = [dot_back(part, down_w) for part in cotangent_rows]
    mine, (gate_w, hidden_grads) = gather_chips(
        (residual_hat * gain_ffn).astype(low), (gate_w, hidden_grads)
    )
    normed_two = mine, lax.ppermute(mine, "shard", sibling)
    hidden, both_grad = [], []
    for j in range(2):
        hidden_grad = hidden_grads[j]
        both = dot(normed_two[j], gate_w)
        gate, upper = both[:, :FF_PAD], both[:, FF_PAD:]
        sigmoid_gate = jax.nn.sigmoid(gate)
        activated = gate * sigmoid_gate
        hidden.append((activated * upper).astype(low))
        both_grad.append(
            jnp.concatenate(
                [
                    hidden_grad * upper * sigmoid_gate * (1.0 + gate * (1.0 - sigmoid_gate)),
                    hidden_grad * activated,
                ],
                axis=1,
            ).astype(low)
        )

    normed_two_grad, (hidden, both_grad) = scatter_rows(
        dot_back(both_grad[0], gate_w), dot_back(both_grad[1], gate_w), (hidden, both_grad)
    )
    gate_grad = sum(map(dot_rows, normed_two, both_grad)).astype(low)
    down_grad = sum(map(dot_rows, hidden, cotangent_rows))[:FF_OWN].astype(low)
    down_grad = down_grad.reshape(reps, own_down, D)
    ffn_grads = jnp.concatenate(
        [
            gate_grad.reshape(reps, block, 2 * FF_PAD),
            jnp.pad(
                down_grad, ((0, 0), (0, down_pad.shape[0] - own_down), (0, 2 * FF_PAD - D))
            ),
        ],
        axis=1,
    )
    normed_two_grad, ffn_grads = lax.optimization_barrier((normed_two_grad, ffn_grads))
    ffn_sums = ffn_grads.reshape(-1, 2 * FF_PAD)
    along_x, along_y = rep_groups(reps)
    ffn_sums = lax.psum_scatter(
        ffn_sums, "rep", scatter_dimension=0, tiled=True, axis_index_groups=along_x
    )
    gain_ffn_grad, residual_part = norm_back(
        normed_two_grad, residual_hat, residual_scale, gain_ffn
    )
    residual_grad = cotangent.astype(wide) + residual_part
    branch_own = residual_grad.astype(low)
    branch_grad = gather_rows(branch_own)
    incoming = [dot_back(part, out_w).astype(low) for part in branch_grad]
    projected_grad, turned_grad, head_gain_grad = attention_backward(
        place, projected, cos, sin, start, gain_heads, query, key, value, shift, incoming
    )
    normed_parts = [dot_back(part, qkv_w) for part in (turned_grad[:half], turned_grad[half:])]
    gain_attn_grad = jnp.sum(dot_back(projected_grad, qkv_w) * inputs_hat, axis=0)
    out_grad = sum(map(dot_rows, mixed, branch_grad)).astype(low)
    qkv_grad = dot_rows(normed, projected_grad).astype(low)
    heads = head_gain_grad[0]
    gain_grad = jnp.concatenate(
        [
            gain_attn_grad,
            heads[:HEAD_SIZE] + heads[HEAD_SIZE : 2 * HEAD_SIZE],
            heads[2 * HEAD_SIZE : 3 * HEAD_SIZE],
            gain_ffn_grad,
        ]
    ).astype(low)
    gain_grad = pad_to(gain_grad.reshape(reps, SHARDS, own_gains), 256, 2)
    last_grads = jnp.concatenate(
        [
            qkv_grad.reshape(reps, block, 256),
            fold(out_grad.reshape(reps, own_out, D)),
            gain_grad,
        ],
        axis=1,
    )
    last_grads, ffn_sums = lax.optimization_barrier((last_grads, ffn_sums))
    ffn_sums = lax.psum_scatter(
        ffn_sums, "rep", scatter_dimension=0, tiled=True, axis_index_groups=along_y
    )
    normed_grad, hidden = scatter_rows(*normed_parts, hidden)
    input_hat, input_scale = norm_pieces(inputs)
    input_part = norm_back(normed_grad, input_hat, input_scale, gain_attn)[1]
    input_grad = residual_grad + input_part
    block_output = residual + scatter_rows(*[dot(part, down_w) for part in hidden])[0]
    last_sums = jnp.sum(
        lax.all_to_all(last_grads, "rep", 0, 0, tiled=True).astype(wide), axis=0
    )
    last_sums, input_grad, block_output, ffn_sums = lax.optimization_barrier(
        (last_sums, input_grad, block_output, ffn_sums)
    )
    ffn_sums = ffn_sums.astype(wide)
    gate_sums, down_sums = ffn_sums[:block], ffn_sums[block:, :D]
    back = lax.all_to_all(
        jnp.concatenate(
            [
                jnp.concatenate(
                    [
                        last_sums[:block].reshape(SHARDS, own, 256),
                        gate_sums.reshape(SHARDS, own, 2 * FF_PAD),
                    ],
                    axis=2,
                ),
                pad_to(
                    last_sums[block + 4 * own_out :].reshape(SHARDS, 1, 256), 256 + 2 * FF_PAD, 2
                ),
            ],
            axis=1,
        ).astype(low),
        "shard", 0, 0, tiled=True,
    ).astype(wide)
    last_back, gate_back = back[:, :, :256], back[:, :own, 256:]
    gain_total = jnp.sum(last_back[:, own, :own_gains], axis=0)
    qkv_total = jnp.concatenate(
        [last_back[s, :own, :128] for s in range(SHARDS)]
        + [last_back[s, :own, 128:192] for s in range(SHARDS)]
        + [last_back[s, :own, 192:] for s in range(SHARDS)],
        axis=1,
    )
    back = lax.ppermute(
        jnp.concatenate(
            [
                unfold(last_sums[block : block + 4 * own_out], D),
                down_sums,
            ],
            axis=0,
        ),
        both_axes,
        to_owner,
    )
    out_total, down_total = back[:own_out], back[own_out : own_out + own_down]
    gate_total = jnp.concatenate(
        [gate_back[s, :, :FF_OWN] for s in range(SHARDS)]
        + [gate_back[s, :, FF_PAD : FF_PAD + FF_OWN] for s in range(SHARDS)],
        axis=1,
    )
    results = []
    for weight, grad, first, second, rate, weight_decay in (
        (qkv_proj, qkv_total, qkv_first, qkv_second, rate_scale * D ** (-0.5), decay),
        (out_proj, out_total, out_first, out_second, rate_scale * WO_FAN ** (-0.5), decay),
        (gate_proj, gate_total, gate_first, gate_second, rate_scale * D ** (-0.5), decay),
        (down_proj, down_total, down_first, down_second, rate_scale * FF ** (-0.5), decay),
        (norm_gains, gain_total, gain_first, gain_second, gain_rate, 0.0),
    ):
        results.extend(adamw(weight, grad, first, second, rate, weight_decay))
    return (block_output, input_grad, *results)


def solution(mesh):
    by_rows = P(("rep", "shard"), None)
    by_entry = P(("rep", "shard"))
    return jax.shard_map(
        local,
        mesh=mesh,
        in_specs=(by_rows, by_rows, P("rep", None)) + ((by_rows,) * 4 + (by_entry,)) * 3,
        out_specs=(by_rows,) * 14 + (by_entry,) * 3,
        check_vma=False,
    )
```

```python
import functools

import jax
import jax.numpy as jnp
from jax import lax
from jax.experimental import pallas as pl
from jax.experimental.pallas import tpu as pltpu
from jax.sharding import PartitionSpec as P

D = 1024
FF = 4608
HEAD_SIZE = 64
STEP = 10
QUERY_FEATURES = 1024
KEY_FEATURES = 512
WO_FAN = 4

norm_eps = 1e-05
theta = 1000000.0
beta_one = 0.9
beta_two = 0.95
adam_eps = 1e-08
decay = 0.1
rate_scale = 2.0
gain_rate = 1.0
masked_score = -1e30

SHARDS = 8
CHIPS = 4
FF_OWN = FF // SHARDS
FF_PAD = 640
ROWS_FF_PAD = 40
QUERY_BLOCK = 256
score_scale = HEAD_SIZE ** (-0.5)
low = jnp.bfloat16
wide = jnp.float32
sibling = [(i, i ^ 1) for i in range(SHARDS)]


def from_chip(k):
    return [(i, ((i // 2 - k) % CHIPS) * 2 + i % 2) for i in range(SHARDS)]


def gather_chips(rows, beside=()):
    parts = [rows] + [None] * (CHIPS - 1)
    for k in (2, 1, 3):
        parts[k] = lax.ppermute(rows, "shard", from_chip(k))
    parts[2], beside = lax.optimization_barrier((parts[2], beside))
    return jnp.concatenate(parts, axis=0), beside


def gather_rows(rows):
    mine = gather_chips(rows)[0]
    return mine, lax.ppermute(mine, "shard", sibling)


def scatter_rows(mine, other, beside=()):
    count = mine.shape[0] // CHIPS
    got = lax.ppermute(other.astype(low), "shard", sibling)
    both = mine + got.astype(wide)
    sent = both.astype(low)
    sent, beside = lax.optimization_barrier((sent, beside))
    total = both[:count]
    for k in (2, 1, 3):
        total = total + lax.ppermute(
            sent[k * count : (k + 1) * count], "shard", from_chip(-k)
        ).astype(wide)
    return total, beside


def norm_pieces(field):
    scale = lax.rsqrt(jnp.mean(field * field, axis=-1, keepdims=True) + norm_eps)
    return field * scale, scale


def norm_back(incoming_grad, normed, scale, gain):
    gain_grad = jnp.sum(incoming_grad * normed, axis=0)
    scaled = incoming_grad * gain
    inner = jnp.mean(scaled * normed, axis=-1, keepdims=True)
    return gain_grad, scale * (scaled - normed * inner)


def sequence_info(lengths_row, index):
    ends = jnp.cumsum(lengths_row)
    passed = ends[None, :] <= index[:, None]
    return jnp.sum(jnp.where(passed, lengths_row[None, :], 0), axis=1)


def rotation_tables(places):
    half = HEAD_SIZE // 2
    freqs = theta ** (-(jnp.arange(half, dtype=wide) * 2.0) / HEAD_SIZE)
    angles = places.astype(wide)[:, None] * freqs[None, :]
    cos, sin = jnp.cos(angles), jnp.sin(angles)
    return jnp.concatenate([cos] * 4, axis=1), jnp.concatenate([-sin, sin, -sin, sin], axis=1)


def lanes(rows):
    return lax.broadcasted_iota(jnp.int32, (rows, 2 * HEAD_SIZE), 1)


def partner(field):
    first = lanes(field.shape[0]) % HEAD_SIZE < HEAD_SIZE // 2
    return jnp.where(first, pltpu.roll(field, 96, 1), pltpu.roll(field, 32, 1))


def left_mean(field):
    left = lanes(field.shape[0]) < HEAD_SIZE
    return jnp.sum(jnp.where(left, field, 0.0), axis=1, keepdims=True) / HEAD_SIZE


def head_means(field):
    left = lanes(field.shape[0]) < HEAD_SIZE
    one = jnp.sum(jnp.where(left, field, 0.0), axis=1, keepdims=True) / HEAD_SIZE
    two = jnp.sum(jnp.where(left, 0.0, field), axis=1, keepdims=True) / HEAD_SIZE
    return jnp.where(left, one, two)


def swap_heads(field):
    return pltpu.roll(field, HEAD_SIZE, 1)


def stack_heads(block):
    left = (lax.broadcasted_iota(jnp.int32, (1, 2 * HEAD_SIZE), 1) < HEAD_SIZE).astype(wide)
    return jnp.concatenate([block * left.astype(low), block * (1.0 - left).astype(low)], axis=0)


def allowed_keys(start_ref, block, keys):
    begin = start_ref[block * QUERY_BLOCK : (block + 1) * QUERY_BLOCK, :]
    begin = jnp.concatenate([begin, begin], axis=0)
    row = lax.broadcasted_iota(jnp.int32, (2 * QUERY_BLOCK, keys), 0)
    row = block * QUERY_BLOCK + jnp.where(row >= QUERY_BLOCK, row - QUERY_BLOCK, row)
    col = lax.broadcasted_iota(jnp.int32, (2 * QUERY_BLOCK, keys), 1)
    return (col >= begin) & (col <= row)


def dot_last(one, two):
    return lax.dot_general(one, two, (((1,), (1,)), ((), ())), preferred_element_type=wide)


def dot_first(one, two):
    return lax.dot_general(one, two, (((0,), (0,)), ((), ())), preferred_element_type=wide)


def forward_kernel(
    place_ref, proj_ref, cos_ref, sin_ref, start_ref, gain_ref,
    out_ref, query_ref, key_ref, value_ref, shift_ref, mixed_ref,
):
    count = proj_ref.shape[0] // SHARDS
    left = lanes(count) < HEAD_SIZE
    gain_query = gain_ref[:, :128]
    gain_key = gain_ref[:, 128:]
    for chunk in range(SHARDS):
        rows = slice(chunk * count, (chunk + 1) * count)
        cos, sin = cos_ref[rows, :], sin_ref[rows, :]
        query = proj_ref[rows, :128]
        query = query * lax.rsqrt(head_means(query * query) + norm_eps) * gain_query
        query = (query * cos + partner(query) * sin).astype(low)
        query_ref[rows, :] = query * jnp.asarray(score_scale, low)
        both = proj_ref[rows, 128:]
        key = both * lax.rsqrt(left_mean(both * both) + norm_eps) * gain_key
        key = key * cos + partner(key) * sin
        both = jnp.where(left, key, both)
        turned = swap_heads(both)
        key_ref[rows, :] = jnp.where(left, both, turned).astype(low)
        value_ref[rows, :] = jnp.where(left, turned, both).astype(low)
    half = lanes(QUERY_BLOCK) < HEAD_SIZE
    for block in range(proj_ref.shape[0] // QUERY_BLOCK):
        keys = (block + 1) * QUERY_BLOCK
        span = slice(block * QUERY_BLOCK, keys)
        query = stack_heads(query_ref[span, :])
        raw = dot_last(query, key_ref[:keys, :])
        raw = jnp.where(allowed_keys(start_ref, block, keys), raw, masked_score)
        top = jnp.max(raw, axis=1, keepdims=True)
        weight = jnp.exp(raw - top)
        total = jnp.sum(weight, axis=1, keepdims=True)
        probs = (weight * (1.0 / total)).astype(low)
        mixed = jnp.dot(probs, value_ref[:keys, :], preferred_element_type=wide)
        mixed_ref[span, :] = jnp.where(half, mixed[:QUERY_BLOCK], mixed[QUERY_BLOCK:])
        shift_ref[2 * block * QUERY_BLOCK : 2 * keys, :] = top + jnp.log(total)
    for chunk in range(SHARDS):
        place = pl.multiple_of(place_ref[chunk], 128)
        out_ref[chunk] = mixed_ref[pl.ds(place, count), :].astype(low)


def backward_kernel(
    place_ref, proj_ref, cos_ref, sin_ref, start_ref, gain_ref, query_ref, key_ref, value_ref,
    shift_ref, in0_ref, in1_ref, out_ref, turned_ref, gain_grad_ref, back_ref, query_grad_ref, key_grad_ref,
    value_grad_ref,
):
    count = proj_ref.shape[0] // SHARDS
    left = lanes(count) < HEAD_SIZE
    gain_query = gain_ref[:, :128]
    gain_key = gain_ref[:, 128:]
    for chunk in range(SHARDS):
        place = pl.multiple_of(place_ref[chunk], 128)
        in_ref = (in0_ref, in1_ref)[chunk // CHIPS]
        part = slice(chunk % CHIPS * count, (chunk % CHIPS + 1) * count)
        back_ref[pl.ds(place, count), :] = in_ref[part, :]
    key_grad_ref[...] = jnp.zeros_like(key_grad_ref)
    value_grad_ref[...] = jnp.zeros_like(value_grad_ref)
    half = lanes(QUERY_BLOCK) < HEAD_SIZE
    for block in range(proj_ref.shape[0] // QUERY_BLOCK):
        keys = (block + 1) * QUERY_BLOCK
        span = slice(block * QUERY_BLOCK, keys)
        query = stack_heads(query_ref[span, :])
        back = stack_heads(back_ref[span, :])
        raw = dot_last(query, key_ref[:keys, :])
        shift = shift_ref[2 * block * QUERY_BLOCK : 2 * keys, :]
        probs = jnp.where(allowed_keys(start_ref, block, keys), jnp.exp(raw - shift), 0.0)
        prob_grad = dot_last(back, value_ref[:keys, :])
        spread = jnp.sum(probs * prob_grad, axis=1, keepdims=True)
        score_grad = (probs * (prob_grad - spread)).astype(low)
        query_grad = jnp.dot(score_grad, key_ref[:keys, :], preferred_element_type=wide)
        query_grad_ref[span, :] = score_scale * jnp.where(
            half, query_grad[:QUERY_BLOCK], query_grad[QUERY_BLOCK:]
        )
        key_grad_ref[:keys, :] += dot_first(score_grad, query)
        value_grad_ref[:keys, :] += dot_first(probs.astype(low), back)
    gain_query_grad = jnp.zeros((1, 128), wide)
    gain_key_grad = jnp.zeros((1, 128), wide)
    for chunk in range(SHARDS):
        rows = slice(chunk * count, (chunk + 1) * count)
        cos, sin = cos_ref[rows, :], sin_ref[rows, :]
        query = proj_ref[rows, :128]
        scale = lax.rsqrt(head_means(query * query) + norm_eps)
        query = query * scale
        grad = query_grad_ref[rows, :]
        grad = grad * cos - partner(grad) * sin
        gain_query_grad += jnp.sum(grad * query, axis=0, keepdims=True)
        grad = grad * gain_query
        out_ref[rows, :128] = (scale * (grad - query * head_means(grad * query))).astype(low)
        key = proj_ref[rows, 128:]
        scale = lax.rsqrt(left_mean(key * key) + norm_eps)
        key = key * scale
        grad = key_grad_ref[rows, :]
        grad = grad + swap_heads(grad)
        grad = grad * cos - partner(grad) * sin
        gain_key_grad += jnp.sum(grad * key, axis=0, keepdims=True)
        grad = grad * gain_key
        grad = scale * (grad - key * left_mean(grad * key))
        value_grad = value_grad_ref[rows, :]
        value_grad = value_grad + swap_heads(value_grad)
        out_ref[rows, 128:] = jnp.where(left, grad, value_grad).astype(low)
    for chunk in range(SHARDS):
        place = pl.multiple_of(place_ref[chunk], 128)
        turned_ref[chunk * count : (chunk + 1) * count, :] = out_ref[pl.ds(place, count), :]
    gain_grad_ref[:, :128] = gain_query_grad
    gain_grad_ref[:, 128:] = gain_key_grad


def in_vmem(count):
    return [pl.BlockSpec(memory_space=pltpu.VMEM)] * count


def attention_forward(place, projected, cos, sin, start, gain):
    rows = cos.shape[0]
    return pl.pallas_call(
        forward_kernel,
        out_shape=[jax.ShapeDtypeStruct((SHARDS, rows // SHARDS, 128), low)]
        + [jax.ShapeDtypeStruct((rows, 128), low)] * 3
        + [jax.ShapeDtypeStruct((2 * rows, 1), wide)],
        in_specs=[pl.BlockSpec(memory_space=pltpu.SMEM)] + in_vmem(5),
        out_specs=in_vmem(5),
        scratch_shapes=[pltpu.VMEM((rows, 128), wide)],
        compiler_params=pltpu.CompilerParams(vmem_limit_bytes=40 * 2**20),
        cost_estimate=pl.CostEstimate(
            flops=10**9, bytes_accessed=5 * 2**20, transcendentals=2 * 10**6
        ),
        name="attention_forward",
    )(place, projected, cos, sin, start, gain)


def attention_backward(place, projected, cos, sin, start, gain, query, key, value, shift, incoming):
    rows = cos.shape[0]
    return pl.pallas_call(
        backward_kernel,
        out_shape=[
            jax.ShapeDtypeStruct((rows, 256), low),
            jax.ShapeDtypeStruct((rows, 256), low),
            jax.ShapeDtypeStruct((1, 256), wide),
        ],
        in_specs=[pl.BlockSpec(memory_space=pltpu.SMEM)] + in_vmem(11),
        out_specs=in_vmem(3),
        scratch_shapes=[pltpu.VMEM((rows, 128), low)] + [pltpu.VMEM((rows, 128), wide)] * 3,
        compiler_params=pltpu.CompilerParams(vmem_limit_bytes=48 * 2**20),
        cost_estimate=pl.CostEstimate(
            flops=3 * 10**9, bytes_accessed=6 * 2**20, transcendentals=2 * 10**6
        ),
        name="attention_backward",
    )(place, projected, cos, sin, start, gain, query, key, value, shift, *incoming)


def copy_kernel(order_ref, in_ref, out_ref):
    out_ref[...] = in_ref[...]


def reorder(order, field, rows):
    width = field.shape[1]
    return pl.pallas_call(
        copy_kernel,
        grid_spec=pltpu.PrefetchScalarGridSpec(
            num_scalar_prefetch=1,
            grid=(SHARDS,),
            in_specs=[pl.BlockSpec((rows, width), lambda i, order: (order[i], 0))],
            out_specs=pl.BlockSpec((rows, width), lambda i, order: (i, 0)),
        ),
        out_shape=jax.ShapeDtypeStruct((SHARDS * rows, width), field.dtype),
        cost_estimate=pl.CostEstimate(flops=0, bytes_accessed=4 * 2**20, transcendentals=0),
        name="reorder",
    )(order, field)


def ffn_kernel(normed_ref, weight_ref, hidden_grad_ref, hidden_ref, both_grad_ref, part_ref):
    width = hidden_ref.shape[1]
    for row in range(0, normed_ref.shape[0], QUERY_BLOCK):
        rows = slice(row, row + QUERY_BLOCK)
        both = jnp.dot(normed_ref[rows, :], weight_ref[...], preferred_element_type=wide)
        gate, upper = both[:, :width], both[:, width:]
        sigmoid_gate = jax.nn.sigmoid(gate)
        activated = gate * sigmoid_gate
        hidden_ref[rows, :] = (activated * upper).astype(low)
        hidden_grad = hidden_grad_ref[rows, :]
        both_grad_ref[rows, :width] = (
            hidden_grad * upper * sigmoid_gate * (1.0 + gate * (1.0 - sigmoid_gate))
        ).astype(low)
        both_grad_ref[rows, width:] = (hidden_grad * activated).astype(low)
        part_ref[rows, :] = dot_last(both_grad_ref[rows, :], weight_ref[...]).astype(part_ref.dtype)


def ffn(normed, weight, hidden_grad, kind):
    rows, width = hidden_grad.shape
    return pl.pallas_call(
        ffn_kernel,
        out_shape=[
            jax.ShapeDtypeStruct((rows, width), low),
            jax.ShapeDtypeStruct((rows, 2 * width), low),
            jax.ShapeDtypeStruct(normed.shape, kind),
        ],
        in_specs=in_vmem(3),
        out_specs=in_vmem(3),
        compiler_params=pltpu.CompilerParams(vmem_limit_bytes=40 * 2**20),
        cost_estimate=pl.CostEstimate(
            flops=3 * 10**9, bytes_accessed=8 * 2**20, transcendentals=10**6
        ),
        name="ffn",
    )(normed, weight, hidden_grad)


def gradient_kernel(
    normed0_ref, normed1_ref, both0_ref, both1_ref, hidden0_ref, hidden1_ref,
    cotangent0_ref, cotangent1_ref, out_ref, down_ref, *, block, own_down,
):
    reps = out_ref.shape[0]
    height = out_ref.shape[1] - block
    width = both0_ref.shape[1]
    for c in range(0, width, 256):
        cols = slice(c, c + 256)
        part = dot_first(normed0_ref[...], both0_ref[:, cols])
        part = part + dot_first(normed1_ref[...], both1_ref[:, cols])
        out_ref[:, :block, cols] = part.astype(low).reshape(reps, block, 256)
    for c in range(0, width, 256):
        cols = slice(c, c + 256)
        if c < D:
            part = dot_first(hidden0_ref[...], cotangent0_ref[:, cols])
            down_ref[...] = part + dot_first(hidden1_ref[...], cotangent1_ref[:, cols])
        else:
            down_ref[...] = jnp.zeros_like(down_ref)
        for r in range(reps):
            out_ref[r, block:, cols] = down_ref[
                r * own_down : r * own_down + height, :
            ].astype(low)


def ffn_gradients(normed, both_grad, hidden, cotangent, reps, block, own_down, height):
    width = both_grad[0].shape[1]
    return pl.pallas_call(
        functools.partial(gradient_kernel, block=block, own_down=own_down),
        out_shape=jax.ShapeDtypeStruct((reps, block + height, width), low),
        in_specs=in_vmem(8),
        out_specs=in_vmem(1)[0],
        scratch_shapes=[pltpu.VMEM((hidden[0].shape[1], 256), wide)],
        compiler_params=pltpu.CompilerParams(vmem_limit_bytes=40 * 2**20),
        cost_estimate=pl.CostEstimate(
            flops=4 * 10**9, bytes_accessed=12 * 2**20, transcendentals=0
        ),
        name="ffn_gradients",
    )(*normed, *both_grad, *hidden, *cotangent)


def adamw(weight, grad, first, second, rate, weight_decay):
    new_first = beta_one * first + (1.0 - beta_one) * grad
    new_second = beta_two * second + (1.0 - beta_two) * grad * grad
    step_size = (
        new_first
        / (1.0 - beta_one**STEP)
        / (jnp.sqrt(new_second / (1.0 - beta_two**STEP)) + adam_eps)
    )
    return (weight - rate * (step_size + weight_decay * weight), new_first, new_second)


def fold(field):
    width = field.shape[-1]
    return jnp.concatenate([field[..., i : i + 256] for i in range(0, width, 256)], axis=-2)


def unfold(field, width):
    count = width // 256
    rows = field.shape[-2] // count
    return jnp.concatenate([field[..., i * rows : (i + 1) * rows, :] for i in range(count)], axis=-1)


def rep_groups(reps):
    side = 4 if reps == 16 else 1
    count = reps // side
    return (
        [[side * x + y for x in range(count)] for y in range(side)],
        [[side * x + y for y in range(side)] for x in range(count)],
    )


def pad_to(field, size, axis):
    widths = [(0, 0)] * field.ndim
    widths[axis] = (0, size - field.shape[axis])
    return jnp.pad(field, widths)


def dot(one, two):
    return jnp.dot(one, two, preferred_element_type=wide)


def dot_back(one, two):
    return jnp.einsum("tc,dc->td", one, two, preferred_element_type=wide)


def dot_rows(one, two):
    return jnp.einsum("td,tc->dc", one, two, preferred_element_type=wide)


def local(
    tokens, cotangent, lengths,
    qkv_proj, out_proj, gate_proj, down_proj, norm_gains,
    qkv_first, out_first, gate_first, down_first, gain_first,
    qkv_second, out_second, gate_second, down_second, gain_second,
):
    reps = lax.axis_size("rep")
    rows = tokens.shape[0]
    half = rows * SHARDS // 2
    own = qkv_proj.shape[0]
    block = own * SHARDS
    own_gains = norm_gains.shape[0]
    own_out = out_proj.shape[0]
    own_down = down_proj.shape[0]
    both_axes = ("rep", "shard")
    to_group = [(s * reps + r, r * SHARDS + s) for r in range(reps) for s in range(SHARDS)]
    to_owner = [(b, a) for a, b in to_group]

    qkv_low = qkv_proj.astype(low)
    qkv_out = jnp.stack(
        [
            jnp.concatenate(
                [
                    qkv_low[:, 128 * s : 128 * s + 128],
                    qkv_low[:, QUERY_FEATURES + 64 * s : QUERY_FEATURES + 64 * s + 64],
                    qkv_low[
                        :,
                        QUERY_FEATURES + KEY_FEATURES + 64 * s : QUERY_FEATURES
                        + KEY_FEATURES
                        + 64 * s
                        + 64,
                    ],
                ],
                axis=1,
            )
            for s in range(SHARDS)
        ]
    )
    gate_low = gate_proj.astype(low)
    gate_out = jnp.stack(
        [
            jnp.concatenate(
                [
                    pad_to(gate_low[:, FF_OWN * s : FF_OWN * (s + 1)], FF_PAD, 1),
                    pad_to(gate_low[:, FF + FF_OWN * s : FF + FF_OWN * (s + 1)], FF_PAD, 1),
                ],
                axis=1,
            )
            for s in range(SHARDS)
        ]
    )
    gain_lanes = -(-own_gains // 128) * 128
    gain_out = jnp.broadcast_to(
        pad_to(pad_to(norm_gains.astype(low)[None, :], gain_lanes, 1), own, 0)[None],
        (SHARDS, own, gain_lanes),
    )
    turned = jnp.concatenate([qkv_out, gate_out, gain_out], axis=2)
    turned = lax.all_to_all(turned, "shard", 0, 0, tiled=True)
    both_rows = lax.all_gather(
        jnp.concatenate([tokens, cotangent], axis=0), "shard", axis=0, tiled=True
    )
    token_rows = both_rows.reshape(SHARDS, 2, rows, D)[:, 0].reshape(2 * half, D)
    down_pad = pad_to(down_proj.astype(low), ROWS_FF_PAD * (own_down // 36), 0)
    moved = lax.ppermute(
        jnp.concatenate([out_proj.astype(low), down_pad], axis=0), both_axes, to_group
    )
    first_parts = jnp.concatenate(
        [
            turned[:, :, :256].reshape(block, 256),
            fold(moved[:own_out]),
            pad_to(turned[:, 0, 1536:], 256, 1),
        ],
        axis=0,
    )
    second_parts = jnp.concatenate(
        [
            turned[:, :, 256:1536].reshape(block, 2 * FF_PAD),
            pad_to(moved[own_out:], 2 * FF_PAD, 1),
        ],
        axis=0,
    )
    second_all = lax.all_gather(second_parts, "rep", axis=0)
    first_all = lax.all_gather(first_parts, "rep", axis=0)
    qkv_w = first_all[:, :block].reshape(D, 256)
    out_w = unfold(first_all[:, block : block + 4 * own_out], D).reshape(reps * own_out, D)
    gains = first_all[:, block + 4 * own_out :, :own_gains].reshape(-1).astype(wide)
    gain_attn = gains[:D]
    gain_query = gains[D : D + HEAD_SIZE]
    gain_key = gains[D + HEAD_SIZE : D + 2 * HEAD_SIZE]
    gain_ffn = gains[D + 2 * HEAD_SIZE :]
    gain_heads = jnp.concatenate([gain_query, gain_query, gain_key, gain_key])[None, :]

    shard_pos = lax.axis_index("shard")
    chip, core = shard_pos // 2, shard_pos % 2
    order = jnp.arange(SHARDS, dtype=jnp.int32)
    place = rows * (2 * ((chip + order % CHIPS) % CHIPS) + (core + order // CHIPS) % 2)
    place = place.astype(jnp.int32)
    index = jnp.arange(rows * SHARDS, dtype=jnp.int32)
    start = sequence_info(lengths[0], index)
    cos, sin = rotation_tables(index - start)
    start = start[:, None]

    inputs_hat = norm_pieces(token_rows.astype(wide))[0]
    normed = (inputs_hat * gain_attn).astype(low)
    projected = dot(normed, qkv_w)
    cotangent_rows = reorder(2 * place // rows + 1, both_rows, rows)
    cotangent_rows = cotangent_rows[:half], cotangent_rows[half:]
    mixed, query, key, value, shift = attention_forward(
        place, projected, cos, sin, start, gain_heads
    )
    mixed = mixed[:CHIPS].reshape(half, 128), mixed[CHIPS:].reshape(half, 128)
    inputs = tokens.astype(wide)
    residual = inputs + scatter_rows(*[dot(part, out_w) for part in mixed])[0]
    residual, second_all = lax.optimization_barrier((residual, second_all))
    gate_w = second_all[:, :block].reshape(D, 2 * FF_PAD)
    down_w = pad_to(second_all[:, block : block + own_down, :D].reshape(FF_OWN, D), FF_PAD, 0)
    residual_hat, residual_scale = norm_pieces(residual)
    hidden_grads = [dot_back(part, down_w) for part in cotangent_rows]
    mine, (gate_w, hidden_grads) = gather_chips(
        (residual_hat * gain_ffn).astype(low), (gate_w, hidden_grads)
    )
    normed_two = mine, lax.ppermute(mine, "shard", sibling)
    hidden, both_grad, parts = zip(
        *[
            ffn(normed_two[j], gate_w, hidden_grads[j], (wide, low)[j])
            for j in range(2)
        ]
    )

    normed_two_grad, (hidden, both_grad) = scatter_rows(*parts, (hidden, both_grad))
    ffn_grads = ffn_gradients(
        normed_two, both_grad, hidden, cotangent_rows, reps, block, own_down, down_pad.shape[0]
    )
    normed_two_grad, ffn_grads = lax.optimization_barrier((normed_two_grad, ffn_grads))
    ffn_sums = ffn_grads.reshape(-1, 2 * FF_PAD)
    along_x, along_y = rep_groups(reps)
    ffn_sums = lax.psum_scatter(
        ffn_sums, "rep", scatter_dimension=0, tiled=True, axis_index_groups=along_x
    )
    gain_ffn_grad, residual_part = norm_back(
        normed_two_grad, residual_hat, residual_scale, gain_ffn
    )
    residual_grad = cotangent.astype(wide) + residual_part
    branch_own = residual_grad.astype(low)
    branch_grad = gather_rows(branch_own)
    incoming = [dot_back(part, out_w).astype(low) for part in branch_grad]
    incoming, hidden = lax.optimization_barrier((incoming, hidden))
    output_part = scatter_rows(*[dot(part, down_w) for part in hidden])[0]
    projected_grad, turned_grad, head_gain_grad = attention_backward(
        place, projected, cos, sin, start, gain_heads, query, key, value, shift, incoming
    )
    normed_parts = [dot_back(part, qkv_w) for part in (turned_grad[:half], turned_grad[half:])]
    gain_attn_grad = jnp.sum(dot_back(projected_grad, qkv_w) * inputs_hat, axis=0)
    out_grad = sum(map(dot_rows, mixed, branch_grad)).astype(low)
    qkv_grad = dot_rows(normed, projected_grad).astype(low)
    heads = head_gain_grad[0]
    gain_grad = jnp.concatenate(
        [
            gain_attn_grad,
            heads[:HEAD_SIZE] + heads[HEAD_SIZE : 2 * HEAD_SIZE],
            heads[2 * HEAD_SIZE : 3 * HEAD_SIZE],
            gain_ffn_grad,
        ]
    ).astype(low)
    gain_grad = pad_to(gain_grad.reshape(reps, SHARDS, own_gains), 256, 2)
    last_grads = jnp.concatenate(
        [
            qkv_grad.reshape(reps, block, 256),
            fold(out_grad.reshape(reps, own_out, D)),
            gain_grad,
        ],
        axis=1,
    )
    normed_grad, (output_part, ffn_sums) = scatter_rows(*normed_parts, (output_part, ffn_sums))
    ffn_sums = lax.psum_scatter(
        ffn_sums, "rep", scatter_dimension=0, tiled=True, axis_index_groups=along_y
    )
    last_sums = jnp.sum(
        lax.all_to_all(last_grads, "rep", 0, 0, tiled=True).astype(wide), axis=0
    )
    normed_grad, last_sums = lax.optimization_barrier((normed_grad, last_sums))
    input_hat, input_scale = norm_pieces(inputs)
    input_part = norm_back(normed_grad, input_hat, input_scale, gain_attn)[1]
    input_grad = residual_grad + input_part
    block_output = residual + output_part
    last_sums, input_grad, block_output, ffn_sums = lax.optimization_barrier(
        (last_sums, input_grad, block_output, ffn_sums)
    )
    ffn_sums = ffn_sums.astype(wide)
    gate_sums, down_sums = ffn_sums[:block], ffn_sums[block:, :D]
    back = lax.all_to_all(
        jnp.concatenate(
            [
                jnp.concatenate(
                    [
                        last_sums[:block].reshape(SHARDS, own, 256),
                        gate_sums.reshape(SHARDS, own, 2 * FF_PAD),
                    ],
                    axis=2,
                ),
                pad_to(
                    last_sums[block + 4 * own_out :].reshape(SHARDS, 1, 256), 256 + 2 * FF_PAD, 2
                ),
            ],
            axis=1,
        ).astype(low),
        "shard", 0, 0, tiled=True,
    ).astype(wide)
    last_back, gate_back = back[:, :, :256], back[:, :own, 256:]
    gain_total = jnp.sum(last_back[:, own, :own_gains], axis=0)
    qkv_total = jnp.concatenate(
        [last_back[s, :own, :128] for s in range(SHARDS)]
        + [last_back[s, :own, 128:192] for s in range(SHARDS)]
        + [last_back[s, :own, 192:] for s in range(SHARDS)],
        axis=1,
    )
    back = lax.ppermute(
        jnp.concatenate(
            [
                unfold(last_sums[block : block + 4 * own_out], D),
                down_sums,
            ],
            axis=0,
        ),
        both_axes,
        to_owner,
    )
    out_total, down_total = back[:own_out], back[own_out : own_out + own_down]
    gate_total = jnp.concatenate(
        [gate_back[s, :, :FF_OWN] for s in range(SHARDS)]
        + [gate_back[s, :, FF_PAD : FF_PAD + FF_OWN] for s in range(SHARDS)],
        axis=1,
    )
    results = []
    for weight, grad, first, second, rate, weight_decay in (
        (qkv_proj, qkv_total, qkv_first, qkv_second, rate_scale * D ** (-0.5), decay),
        (out_proj, out_total, out_first, out_second, rate_scale * WO_FAN ** (-0.5), decay),
        (gate_proj, gate_total, gate_first, gate_second, rate_scale * D ** (-0.5), decay),
        (down_proj, down_total, down_first, down_second, rate_scale * FF ** (-0.5), decay),
        (norm_gains, gain_total, gain_first, gain_second, gain_rate, 0.0),
    ):
        results.extend(adamw(weight, grad, first, second, rate, weight_decay))
    return (block_output, input_grad, *results)


def solution(mesh):
    by_rows = P(("rep", "shard"), None)
    by_entry = P(("rep", "shard"))
    return jax.shard_map(
        local,
        mesh=mesh,
        in_specs=(by_rows, by_rows, P("rep", None)) + ((by_rows,) * 4 + (by_entry,)) * 3,
        out_specs=(by_rows,) * 14 + (by_entry,) * 3,
        check_vma=False,
    )
```

```python
import functools

import jax
import jax.numpy as jnp
from jax import lax
from jax.experimental import pallas as pl
from jax.experimental.pallas import tpu as pltpu
from jax.sharding import PartitionSpec as P

D = 1024
FF = 4608
HEAD_SIZE = 64
STEP = 10
QUERY_FEATURES = 1024
KEY_FEATURES = 512
WO_FAN = 4

norm_eps = 1e-05
theta = 1000000.0
beta_one = 0.9
beta_two = 0.95
adam_eps = 1e-08
decay = 0.1
rate_scale = 2.0
gain_rate = 1.0
masked_score = -1e30

SHARDS = 8
CHIPS = 4
FF_OWN = FF // SHARDS
FF_PAD = 640
ROWS_FF_PAD = 40
QUERY_BLOCK = 256
score_scale = HEAD_SIZE ** (-0.5)
low = jnp.bfloat16
wide = jnp.float32
sibling = [(i, i ^ 1) for i in range(SHARDS)]


def from_chip(k):
    return [(i, ((i // 2 - k) % CHIPS) * 2 + i % 2) for i in range(SHARDS)]


def gather_chips(rows, beside=()):
    parts = [rows] + [None] * (CHIPS - 1)
    for k in (2, 1, 3):
        parts[k] = lax.ppermute(rows, "shard", from_chip(k))
    parts[2], beside = lax.optimization_barrier((parts[2], beside))
    return jnp.concatenate(parts, axis=0), beside


def gather_rows(rows):
    mine = gather_chips(rows)[0]
    return mine, lax.ppermute(mine, "shard", sibling)


def scatter_rows(mine, other, beside=()):
    count = mine.shape[0] // CHIPS
    got = lax.ppermute(other.astype(low), "shard", sibling)
    both = mine + got.astype(wide)
    sent = both.astype(low)
    sent, beside = lax.optimization_barrier((sent, beside))
    total = both[:count]
    for k in (2, 1, 3):
        total = total + lax.ppermute(
            sent[k * count : (k + 1) * count], "shard", from_chip(-k)
        ).astype(wide)
    return total, beside


def norm_pieces(field):
    scale = lax.rsqrt(jnp.mean(field * field, axis=-1, keepdims=True) + norm_eps)
    return field * scale, scale


def norm_back(incoming_grad, normed, scale, gain):
    gain_grad = jnp.sum(incoming_grad * normed, axis=0)
    scaled = incoming_grad * gain
    inner = jnp.mean(scaled * normed, axis=-1, keepdims=True)
    return gain_grad, scale * (scaled - normed * inner)


def sequence_info(lengths_row, index):
    ends = jnp.cumsum(lengths_row)
    passed = ends[None, :] <= index[:, None]
    return jnp.sum(jnp.where(passed, lengths_row[None, :], 0), axis=1)


def rotation_tables(places):
    half = HEAD_SIZE // 2
    freqs = theta ** (-(jnp.arange(half, dtype=wide) * 2.0) / HEAD_SIZE)
    angles = places.astype(wide)[:, None] * freqs[None, :]
    cos, sin = jnp.cos(angles), jnp.sin(angles)
    return jnp.concatenate([cos] * 4, axis=1), jnp.concatenate([-sin, sin, -sin, sin], axis=1)


def lanes(rows):
    return lax.broadcasted_iota(jnp.int32, (rows, 2 * HEAD_SIZE), 1)


def partner(field):
    first = lanes(field.shape[0]) % HEAD_SIZE < HEAD_SIZE // 2
    return jnp.where(first, pltpu.roll(field, 96, 1), pltpu.roll(field, 32, 1))


def left_mean(field):
    left = lanes(field.shape[0]) < HEAD_SIZE
    return jnp.sum(jnp.where(left, field, 0.0), axis=1, keepdims=True) / HEAD_SIZE


def head_means(field):
    left = lanes(field.shape[0]) < HEAD_SIZE
    one = jnp.sum(jnp.where(left, field, 0.0), axis=1, keepdims=True) / HEAD_SIZE
    two = jnp.sum(jnp.where(left, 0.0, field), axis=1, keepdims=True) / HEAD_SIZE
    return jnp.where(left, one, two)


def swap_heads(field):
    return pltpu.roll(field, HEAD_SIZE, 1)


def stack_heads(block):
    left = (lax.broadcasted_iota(jnp.int32, (1, 2 * HEAD_SIZE), 1) < HEAD_SIZE).astype(wide)
    return jnp.concatenate([block * left.astype(low), block * (1.0 - left).astype(low)], axis=0)


def allowed_keys(start_ref, block, keys):
    begin = start_ref[block * QUERY_BLOCK : (block + 1) * QUERY_BLOCK, :]
    begin = jnp.concatenate([begin, begin], axis=0)
    row = lax.broadcasted_iota(jnp.int32, (2 * QUERY_BLOCK, keys), 0)
    row = block * QUERY_BLOCK + jnp.where(row >= QUERY_BLOCK, row - QUERY_BLOCK, row)
    col = lax.broadcasted_iota(jnp.int32, (2 * QUERY_BLOCK, keys), 1)
    return (col >= begin) & (col <= row)


def dot_last(one, two):
    return lax.dot_general(one, two, (((1,), (1,)), ((), ())), preferred_element_type=wide)


def dot_first(one, two):
    return lax.dot_general(one, two, (((0,), (0,)), ((), ())), preferred_element_type=wide)


def forward_kernel(
    place_ref, proj_ref, cos_ref, sin_ref, start_ref, gain_ref,
    out_ref, query_ref, key_ref, value_ref, shift_ref, mixed_ref,
):
    count = proj_ref.shape[0] // SHARDS
    left = lanes(count) < HEAD_SIZE
    gain_query = gain_ref[:, :128]
    gain_key = gain_ref[:, 128:]
    for chunk in range(SHARDS):
        rows = slice(chunk * count, (chunk + 1) * count)
        cos, sin = cos_ref[rows, :], sin_ref[rows, :]
        query = proj_ref[rows, :128]
        query = query * lax.rsqrt(head_means(query * query) + norm_eps) * gain_query
        query = (query * cos + partner(query) * sin).astype(low)
        query_ref[rows, :] = query * jnp.asarray(score_scale, low)
        both = proj_ref[rows, 128:]
        key = both * lax.rsqrt(left_mean(both * both) + norm_eps) * gain_key
        key = key * cos + partner(key) * sin
        both = jnp.where(left, key, both)
        turned = swap_heads(both)
        key_ref[rows, :] = jnp.where(left, both, turned).astype(low)
        value_ref[rows, :] = jnp.where(left, turned, both).astype(low)
    half = lanes(QUERY_BLOCK) < HEAD_SIZE
    for block in range(proj_ref.shape[0] // QUERY_BLOCK):
        keys = (block + 1) * QUERY_BLOCK
        span = slice(block * QUERY_BLOCK, keys)
        query = stack_heads(query_ref[span, :])
        raw = dot_last(query, key_ref[:keys, :])
        raw = jnp.where(allowed_keys(start_ref, block, keys), raw, masked_score)
        top = jnp.max(raw, axis=1, keepdims=True)
        weight = jnp.exp(raw - top)
        total = jnp.sum(weight, axis=1, keepdims=True)
        probs = (weight * (1.0 / total)).astype(low)
        mixed = jnp.dot(probs, value_ref[:keys, :], preferred_element_type=wide)
        mixed_ref[span, :] = jnp.where(half, mixed[:QUERY_BLOCK], mixed[QUERY_BLOCK:])
        shift_ref[2 * block * QUERY_BLOCK : 2 * keys, :] = top + jnp.log(total)
    for chunk in range(SHARDS):
        place = pl.multiple_of(place_ref[chunk], 128)
        out_ref[chunk] = mixed_ref[pl.ds(place, count), :].astype(low)


def backward_kernel(
    place_ref, proj_ref, cos_ref, sin_ref, start_ref, gain_ref, query_ref, key_ref, value_ref,
    shift_ref, in0_ref, in1_ref, out_ref, turned_ref, gain_grad_ref, back_ref, query_grad_ref, key_grad_ref,
    value_grad_ref,
):
    count = proj_ref.shape[0] // SHARDS
    left = lanes(count) < HEAD_SIZE
    gain_query = gain_ref[:, :128]
    gain_key = gain_ref[:, 128:]
    for chunk in range(SHARDS):
        place = pl.multiple_of(place_ref[chunk], 128)
        in_ref = (in0_ref, in1_ref)[chunk // CHIPS]
        part = slice(chunk % CHIPS * count, (chunk % CHIPS + 1) * count)
        back_ref[pl.ds(place, count), :] = in_ref[part, :]
    key_grad_ref[...] = jnp.zeros_like(key_grad_ref)
    value_grad_ref[...] = jnp.zeros_like(value_grad_ref)
    half = lanes(QUERY_BLOCK) < HEAD_SIZE
    for block in range(proj_ref.shape[0] // QUERY_BLOCK):
        keys = (block + 1) * QUERY_BLOCK
        span = slice(block * QUERY_BLOCK, keys)
        query = stack_heads(query_ref[span, :])
        back = stack_heads(back_ref[span, :])
        raw = dot_last(query, key_ref[:keys, :])
        shift = shift_ref[2 * block * QUERY_BLOCK : 2 * keys, :]
        probs = jnp.where(allowed_keys(start_ref, block, keys), jnp.exp(raw - shift), 0.0)
        prob_grad = dot_last(back, value_ref[:keys, :])
        spread = jnp.sum(probs * prob_grad, axis=1, keepdims=True)
        score_grad = (probs * (prob_grad - spread)).astype(low)
        query_grad = jnp.dot(score_grad, key_ref[:keys, :], preferred_element_type=wide)
        query_grad_ref[span, :] = score_scale * jnp.where(
            half, query_grad[:QUERY_BLOCK], query_grad[QUERY_BLOCK:]
        )
        key_grad_ref[:keys, :] += dot_first(score_grad, query)
        value_grad_ref[:keys, :] += dot_first(probs.astype(low), back)
    gain_query_grad = jnp.zeros((1, 128), wide)
    gain_key_grad = jnp.zeros((1, 128), wide)
    for chunk in range(SHARDS):
        rows = slice(chunk * count, (chunk + 1) * count)
        cos, sin = cos_ref[rows, :], sin_ref[rows, :]
        query = proj_ref[rows, :128]
        scale = lax.rsqrt(head_means(query * query) + norm_eps)
        query = query * scale
        grad = query_grad_ref[rows, :]
        grad = grad * cos - partner(grad) * sin
        gain_query_grad += jnp.sum(grad * query, axis=0, keepdims=True)
        grad = grad * gain_query
        out_ref[rows, :128] = (scale * (grad - query * head_means(grad * query))).astype(low)
        key = proj_ref[rows, 128:]
        scale = lax.rsqrt(left_mean(key * key) + norm_eps)
        key = key * scale
        grad = key_grad_ref[rows, :]
        grad = grad + swap_heads(grad)
        grad = grad * cos - partner(grad) * sin
        gain_key_grad += jnp.sum(grad * key, axis=0, keepdims=True)
        grad = grad * gain_key
        grad = scale * (grad - key * left_mean(grad * key))
        value_grad = value_grad_ref[rows, :]
        value_grad = value_grad + swap_heads(value_grad)
        out_ref[rows, 128:] = jnp.where(left, grad, value_grad).astype(low)
    for chunk in range(SHARDS):
        place = pl.multiple_of(place_ref[chunk], 128)
        turned_ref[chunk * count : (chunk + 1) * count, :] = out_ref[pl.ds(place, count), :]
    gain_grad_ref[:, :128] = gain_query_grad
    gain_grad_ref[:, 128:] = gain_key_grad


def in_vmem(count):
    return [pl.BlockSpec(memory_space=pltpu.VMEM)] * count


def attention_forward(place, projected, cos, sin, start, gain):
    rows = cos.shape[0]
    return pl.pallas_call(
        forward_kernel,
        out_shape=[jax.ShapeDtypeStruct((SHARDS, rows // SHARDS, 128), low)]
        + [jax.ShapeDtypeStruct((rows, 128), low)] * 3
        + [jax.ShapeDtypeStruct((2 * rows, 1), wide)],
        in_specs=[pl.BlockSpec(memory_space=pltpu.SMEM)] + in_vmem(5),
        out_specs=in_vmem(5),
        scratch_shapes=[pltpu.VMEM((rows, 128), wide)],
        compiler_params=pltpu.CompilerParams(vmem_limit_bytes=40 * 2**20),
        cost_estimate=pl.CostEstimate(
            flops=10**9, bytes_accessed=5 * 2**20, transcendentals=2 * 10**6
        ),
        name="attention_forward",
    )(place, projected, cos, sin, start, gain)


def attention_backward(place, projected, cos, sin, start, gain, query, key, value, shift, incoming):
    rows = cos.shape[0]
    return pl.pallas_call(
        backward_kernel,
        out_shape=[
            jax.ShapeDtypeStruct((rows, 256), low),
            jax.ShapeDtypeStruct((rows, 256), low),
            jax.ShapeDtypeStruct((1, 256), wide),
        ],
        in_specs=[pl.BlockSpec(memory_space=pltpu.SMEM)] + in_vmem(11),
        out_specs=in_vmem(3),
        scratch_shapes=[pltpu.VMEM((rows, 128), low)] + [pltpu.VMEM((rows, 128), wide)] * 3,
        compiler_params=pltpu.CompilerParams(vmem_limit_bytes=48 * 2**20),
        cost_estimate=pl.CostEstimate(
            flops=3 * 10**9, bytes_accessed=6 * 2**20, transcendentals=2 * 10**6
        ),
        name="attention_backward",
    )(place, projected, cos, sin, start, gain, query, key, value, shift, *incoming)


def copy_kernel(order_ref, in_ref, out_ref):
    out_ref[...] = in_ref[...]


def reorder(order, field, rows):
    width = field.shape[1]
    return pl.pallas_call(
        copy_kernel,
        grid_spec=pltpu.PrefetchScalarGridSpec(
            num_scalar_prefetch=1,
            grid=(SHARDS,),
            in_specs=[pl.BlockSpec((rows, width), lambda i, order: (order[i], 0))],
            out_specs=pl.BlockSpec((rows, width), lambda i, order: (i, 0)),
        ),
        out_shape=jax.ShapeDtypeStruct((SHARDS * rows, width), field.dtype),
        cost_estimate=pl.CostEstimate(flops=0, bytes_accessed=4 * 2**20, transcendentals=0),
        name="reorder",
    )(order, field)


def ffn_kernel(normed_ref, weight_ref, hidden_grad_ref, hidden_ref, both_grad_ref, part_ref):
    width = hidden_ref.shape[1]
    for row in range(0, normed_ref.shape[0], QUERY_BLOCK):
        rows = slice(row, row + QUERY_BLOCK)
        both = jnp.dot(normed_ref[rows, :], weight_ref[...], preferred_element_type=wide)
        gate, upper = both[:, :width], both[:, width:]
        sigmoid_gate = jax.nn.sigmoid(gate)
        activated = gate * sigmoid_gate
        hidden_ref[rows, :] = (activated * upper).astype(low)
        hidden_grad = hidden_grad_ref[rows, :]
        both_grad_ref[rows, :width] = (
            hidden_grad * upper * sigmoid_gate * (1.0 + gate * (1.0 - sigmoid_gate))
        ).astype(low)
        both_grad_ref[rows, width:] = (hidden_grad * activated).astype(low)
        part_ref[rows, :] = dot_last(both_grad_ref[rows, :], weight_ref[...]).astype(part_ref.dtype)


def ffn(normed, weight, hidden_grad, kind):
    rows, width = hidden_grad.shape
    return pl.pallas_call(
        ffn_kernel,
        out_shape=[
            jax.ShapeDtypeStruct((rows, width), low),
            jax.ShapeDtypeStruct((rows, 2 * width), low),
            jax.ShapeDtypeStruct(normed.shape, kind),
        ],
        in_specs=in_vmem(3),
        out_specs=in_vmem(3),
        compiler_params=pltpu.CompilerParams(vmem_limit_bytes=40 * 2**20),
        cost_estimate=pl.CostEstimate(
            flops=3 * 10**9, bytes_accessed=8 * 2**20, transcendentals=10**6
        ),
        name="ffn",
    )(normed, weight, hidden_grad)


def gradient_kernel(
    normed0_ref, normed1_ref, both0_ref, both1_ref, hidden0_ref, hidden1_ref,
    cotangent0_ref, cotangent1_ref, out_ref, down_ref, *, block, own_down,
):
    reps = out_ref.shape[0]
    height = out_ref.shape[1] - block
    width = both0_ref.shape[1]
    for c in range(0, width, 256):
        cols = slice(c, c + 256)
        part = dot_first(normed0_ref[...], both0_ref[:, cols])
        part = part + dot_first(normed1_ref[...], both1_ref[:, cols])
        out_ref[:, :block, cols] = part.astype(low).reshape(reps, block, 256)
    for c in range(0, width, 256):
        cols = slice(c, c + 256)
        if c < D:
            part = dot_first(hidden0_ref[...], cotangent0_ref[:, cols])
            down_ref[...] = part + dot_first(hidden1_ref[...], cotangent1_ref[:, cols])
        else:
            down_ref[...] = jnp.zeros_like(down_ref)
        for r in range(reps):
            out_ref[r, block:, cols] = down_ref[
                r * own_down : r * own_down + height, :
            ].astype(low)


def ffn_gradients(normed, both_grad, hidden, cotangent, reps, block, own_down, height):
    width = both_grad[0].shape[1]
    return pl.pallas_call(
        functools.partial(gradient_kernel, block=block, own_down=own_down),
        out_shape=jax.ShapeDtypeStruct((reps, block + height, width), low),
        in_specs=in_vmem(8),
        out_specs=in_vmem(1)[0],
        scratch_shapes=[pltpu.VMEM((hidden[0].shape[1], 256), wide)],
        compiler_params=pltpu.CompilerParams(vmem_limit_bytes=40 * 2**20),
        cost_estimate=pl.CostEstimate(
            flops=4 * 10**9, bytes_accessed=12 * 2**20, transcendentals=0
        ),
        name="ffn_gradients",
    )(*normed, *both_grad, *hidden, *cotangent)


def adamw(weight, grad, first, second, rate, weight_decay):
    new_first = beta_one * first + (1.0 - beta_one) * grad
    new_second = beta_two * second + (1.0 - beta_two) * grad * grad
    step_size = (
        new_first
        / (1.0 - beta_one**STEP)
        / (jnp.sqrt(new_second / (1.0 - beta_two**STEP)) + adam_eps)
    )
    return (weight - rate * (step_size + weight_decay * weight), new_first, new_second)


def fold(field):
    width = field.shape[-1]
    return jnp.concatenate([field[..., i : i + 256] for i in range(0, width, 256)], axis=-2)


def unfold(field, width):
    count = width // 256
    rows = field.shape[-2] // count
    return jnp.concatenate([field[..., i * rows : (i + 1) * rows, :] for i in range(count)], axis=-1)


def rep_groups(reps):
    side = 4 if reps == 16 else 1
    count = reps // side
    return (
        [[side * x + y for x in range(count)] for y in range(side)],
        [[side * x + y for y in range(side)] for x in range(count)],
    )


def pad_to(field, size, axis):
    widths = [(0, 0)] * field.ndim
    widths[axis] = (0, size - field.shape[axis])
    return jnp.pad(field, widths)


def dot(one, two):
    return jnp.dot(one, two, preferred_element_type=wide)


def dot_back(one, two):
    return jnp.einsum("tc,dc->td", one, two, preferred_element_type=wide)


def dot_rows(one, two):
    return jnp.einsum("td,tc->dc", one, two, preferred_element_type=wide)


def local(
    tokens, cotangent, lengths,
    qkv_proj, out_proj, gate_proj, down_proj, norm_gains,
    qkv_first, out_first, gate_first, down_first, gain_first,
    qkv_second, out_second, gate_second, down_second, gain_second,
):
    reps = lax.axis_size("rep")
    rows = tokens.shape[0]
    half = rows * SHARDS // 2
    own = qkv_proj.shape[0]
    block = own * SHARDS
    own_gains = norm_gains.shape[0]
    own_out = out_proj.shape[0]
    own_down = down_proj.shape[0]
    both_axes = ("rep", "shard")
    to_group = [(s * reps + r, r * SHARDS + s) for r in range(reps) for s in range(SHARDS)]
    to_owner = [(b, a) for a, b in to_group]

    qkv_low = qkv_proj.astype(low)
    qkv_out = jnp.stack(
        [
            jnp.concatenate(
                [
                    qkv_low[:, 128 * s : 128 * s + 128],
                    qkv_low[:, QUERY_FEATURES + 64 * s : QUERY_FEATURES + 64 * s + 64],
                    qkv_low[
                        :,
                        QUERY_FEATURES + KEY_FEATURES + 64 * s : QUERY_FEATURES
                        + KEY_FEATURES
                        + 64 * s
                        + 64,
                    ],
                ],
                axis=1,
            )
            for s in range(SHARDS)
        ]
    )
    gate_low = gate_proj.astype(low)
    gate_out = jnp.stack(
        [
            jnp.concatenate(
                [
                    pad_to(gate_low[:, FF_OWN * s : FF_OWN * (s + 1)], FF_PAD, 1),
                    pad_to(gate_low[:, FF + FF_OWN * s : FF + FF_OWN * (s + 1)], FF_PAD, 1),
                ],
                axis=1,
            )
            for s in range(SHARDS)
        ]
    )
    gain_lanes = -(-own_gains // 128) * 128
    gain_out = jnp.broadcast_to(
        pad_to(pad_to(norm_gains.astype(low)[None, :], gain_lanes, 1), own, 0)[None],
        (SHARDS, own, gain_lanes),
    )
    turned = jnp.concatenate([qkv_out, gate_out, gain_out], axis=2)
    turned = lax.all_to_all(turned, "shard", 0, 0, tiled=True)
    both_rows = lax.all_gather(
        jnp.concatenate([tokens, cotangent], axis=0), "shard", axis=0, tiled=True
    )
    token_rows = both_rows.reshape(SHARDS, 2, rows, D)[:, 0].reshape(2 * half, D)
    down_pad = pad_to(down_proj.astype(low), ROWS_FF_PAD * (own_down // 36), 0)
    moved = lax.ppermute(
        jnp.concatenate([out_proj.astype(low), down_pad], axis=0), both_axes, to_group
    )
    first_parts = jnp.concatenate(
        [
            turned[:, :, :256].reshape(block, 256),
            fold(moved[:own_out]),
            pad_to(turned[:, 0, 1536:], 256, 1),
        ],
        axis=0,
    )
    second_parts = jnp.concatenate(
        [
            turned[:, :, 256:1536].reshape(block, 2 * FF_PAD),
            pad_to(moved[own_out:], 2 * FF_PAD, 1),
        ],
        axis=0,
    )
    second_all = lax.all_gather(second_parts, "rep", axis=0)
    first_all = lax.all_gather(first_parts, "rep", axis=0)
    qkv_w = first_all[:, :block].reshape(D, 256)
    out_w = unfold(first_all[:, block : block + 4 * own_out], D).reshape(reps * own_out, D)
    gains = first_all[:, block + 4 * own_out :, :own_gains].reshape(-1).astype(wide)
    gain_attn = gains[:D]
    gain_query = gains[D : D + HEAD_SIZE]
    gain_key = gains[D + HEAD_SIZE : D + 2 * HEAD_SIZE]
    gain_ffn = gains[D + 2 * HEAD_SIZE :]
    gain_heads = jnp.concatenate([gain_query, gain_query, gain_key, gain_key])[None, :]

    shard_pos = lax.axis_index("shard")
    chip, core = shard_pos // 2, shard_pos % 2
    order = jnp.arange(SHARDS, dtype=jnp.int32)
    place = rows * (2 * ((chip + order % CHIPS) % CHIPS) + (core + order // CHIPS) % 2)
    place = place.astype(jnp.int32)
    index = jnp.arange(rows * SHARDS, dtype=jnp.int32)
    start = sequence_info(lengths[0], index)
    cos, sin = rotation_tables(index - start)
    start = start[:, None]

    inputs_hat = norm_pieces(token_rows.astype(wide))[0]
    normed = (inputs_hat * gain_attn).astype(low)
    projected = dot(normed, qkv_w)
    cotangent_rows = reorder(2 * place // rows + 1, both_rows, rows)
    cotangent_rows = cotangent_rows[:half], cotangent_rows[half:]
    mixed, query, key, value, shift = attention_forward(
        place, projected, cos, sin, start, gain_heads
    )
    mixed = mixed[:CHIPS].reshape(half, 128), mixed[CHIPS:].reshape(half, 128)
    inputs = tokens.astype(wide)
    residual = inputs + scatter_rows(*[dot(part, out_w) for part in mixed])[0]
    residual, second_all = lax.optimization_barrier((residual, second_all))
    gate_w = second_all[:, :block].reshape(D, 2 * FF_PAD)
    down_w = pad_to(second_all[:, block : block + own_down, :D].reshape(FF_OWN, D), FF_PAD, 0)
    residual_hat, residual_scale = norm_pieces(residual)
    hidden_grads = [dot_back(part, down_w) for part in cotangent_rows]
    mine, (gate_w, hidden_grads) = gather_chips(
        (residual_hat * gain_ffn).astype(low), (gate_w, hidden_grads)
    )
    normed_two = mine, lax.ppermute(mine, "shard", sibling)
    hidden, both_grad, parts = zip(
        *[
            ffn(normed_two[j], gate_w, hidden_grads[j], (wide, low)[j])
            for j in range(2)
        ]
    )

    normed_two_grad, (hidden, both_grad) = scatter_rows(*parts, (hidden, both_grad))
    ffn_grads = ffn_gradients(
        normed_two, both_grad, hidden, cotangent_rows, reps, block, own_down, down_pad.shape[0]
    )
    normed_two_grad, ffn_grads = lax.optimization_barrier((normed_two_grad, ffn_grads))
    ffn_sums = ffn_grads.reshape(-1, 2 * FF_PAD)
    along_x, along_y = rep_groups(reps)
    ffn_sums = lax.psum_scatter(
        ffn_sums, "rep", scatter_dimension=0, tiled=True, axis_index_groups=along_x
    )
    gain_ffn_grad, residual_part = norm_back(
        normed_two_grad, residual_hat, residual_scale, gain_ffn
    )
    residual_grad = cotangent.astype(wide) + residual_part
    branch_own = residual_grad.astype(low)
    branch_grad = gather_rows(branch_own)
    incoming = [dot_back(part, out_w).astype(low) for part in branch_grad]
    incoming, hidden = lax.optimization_barrier((incoming, hidden))
    output_part = scatter_rows(*[dot(part, down_w) for part in hidden])[0]
    projected_grad, turned_grad, head_gain_grad = attention_backward(
        place, projected, cos, sin, start, gain_heads, query, key, value, shift, incoming
    )
    normed_parts = [dot_back(part, qkv_w) for part in (turned_grad[:half], turned_grad[half:])]
    gain_attn_grad = jnp.sum(dot_back(projected_grad, qkv_w) * inputs_hat, axis=0)
    out_grad = sum(map(dot_rows, mixed, branch_grad)).astype(low)
    qkv_grad = dot_rows(normed, projected_grad).astype(low)
    heads = head_gain_grad[0]
    gain_grad = jnp.concatenate(
        [
            gain_attn_grad,
            heads[:HEAD_SIZE] + heads[HEAD_SIZE : 2 * HEAD_SIZE],
            heads[2 * HEAD_SIZE : 3 * HEAD_SIZE],
            gain_ffn_grad,
        ]
    ).astype(low)
    gain_grad = pad_to(gain_grad.reshape(reps, SHARDS, own_gains), 256, 2)
    last_grads = jnp.concatenate(
        [
            qkv_grad.reshape(reps, block, 256),
            fold(out_grad.reshape(reps, own_out, D)),
            gain_grad,
        ],
        axis=1,
    )
    normed_grad, ffn_sums = scatter_rows(*normed_parts, ffn_sums)
    ffn_sums = lax.psum_scatter(
        ffn_sums, "rep", scatter_dimension=0, tiled=True, axis_index_groups=along_y
    )
    last_sums = jnp.sum(
        lax.all_to_all(last_grads, "rep", 0, 0, tiled=True).astype(wide), axis=0
    )
    normed_grad, output_part, last_sums = lax.optimization_barrier(
        (normed_grad, output_part, last_sums)
    )
    input_hat, input_scale = norm_pieces(inputs)
    input_part = norm_back(normed_grad, input_hat, input_scale, gain_attn)[1]
    input_grad = residual_grad + input_part
    block_output = residual + output_part
    last_sums, input_grad, block_output, ffn_sums = lax.optimization_barrier(
        (last_sums, input_grad, block_output, ffn_sums)
    )
    ffn_sums = ffn_sums.astype(wide)
    gate_sums, down_sums = ffn_sums[:block], ffn_sums[block:, :D]
    back = lax.all_to_all(
        jnp.concatenate(
            [
                jnp.concatenate(
                    [
                        last_sums[:block].reshape(SHARDS, own, 256),
                        gate_sums.reshape(SHARDS, own, 2 * FF_PAD),
                    ],
                    axis=2,
                ),
                pad_to(
                    last_sums[block + 4 * own_out :].reshape(SHARDS, 1, 256), 256 + 2 * FF_PAD, 2
                ),
            ],
            axis=1,
        ).astype(low),
        "shard", 0, 0, tiled=True,
    ).astype(wide)
    last_back, gate_back = back[:, :, :256], back[:, :own, 256:]
    gain_total = jnp.sum(last_back[:, own, :own_gains], axis=0)
    qkv_total = jnp.concatenate(
        [last_back[s, :own, :128] for s in range(SHARDS)]
        + [last_back[s, :own, 128:192] for s in range(SHARDS)]
        + [last_back[s, :own, 192:] for s in range(SHARDS)],
        axis=1,
    )
    back = lax.ppermute(
        jnp.concatenate(
            [
                unfold(last_sums[block : block + 4 * own_out], D).astype(low),
                down_sums.astype(low),
            ],
            axis=0,
        ),
        both_axes,
        to_owner,
    ).astype(wide)
    out_total, down_total = back[:own_out], back[own_out : own_out + own_down]
    gate_total = jnp.concatenate(
        [gate_back[s, :, :FF_OWN] for s in range(SHARDS)]
        + [gate_back[s, :, FF_PAD : FF_PAD + FF_OWN] for s in range(SHARDS)],
        axis=1,
    )
    results = []
    for weight, grad, first, second, rate, weight_decay in (
        (qkv_proj, qkv_total, qkv_first, qkv_second, rate_scale * D ** (-0.5), decay),
        (out_proj, out_total, out_first, out_second, rate_scale * WO_FAN ** (-0.5), decay),
        (gate_proj, gate_total, gate_first, gate_second, rate_scale * D ** (-0.5), decay),
        (down_proj, down_total, down_first, down_second, rate_scale * FF ** (-0.5), decay),
        (norm_gains, gain_total, gain_first, gain_second, gain_rate, 0.0),
    ):
        results.extend(adamw(weight, grad, first, second, rate, weight_decay))
    return (block_output, input_grad, *results)


def solution(mesh):
    by_rows = P(("rep", "shard"), None)
    by_entry = P(("rep", "shard"))
    return jax.shard_map(
        local,
        mesh=mesh,
        in_specs=(by_rows, by_rows, P("rep", None)) + ((by_rows,) * 4 + (by_entry,)) * 3,
        out_specs=(by_rows,) * 14 + (by_entry,) * 3,
        check_vma=False,
    )
```
